256 devices in a mesh: dp: 4 (over x), neuron: 8 (over z), expert: 8 (over y, core).
Axes of the slice: x: 4, y: 4, z: 8, core: 2. Of those that a mesh axis runs over, the one named last changes fastest.
Arguments:
- tokens: bfloat16 [512, 8192], P(('neuron', 'expert'), 'dp'), may hold values from -6 to 6
- teacher_gate: bfloat16 [28672, 8192], P(('neuron', 'expert'), 'dp'), may hold values from -0.0625 to 0.0625
- teacher_up: bfloat16 [28672, 8192], P(('neuron', 'expert'), 'dp'), may hold values from -0.0625 to 0.0625
- teacher_down: bfloat16 [28672, 8192], P(('neuron', 'expert'), 'dp'), may hold values from -0.03125 to 0.03125
- student_gate: bfloat16 [8, 1792, 8192], P('expert', 'neuron', 'dp'), may hold values from -0.0625 to 0.0625
- student_up: bfloat16 [8, 1792, 8192], P('expert', 'neuron', 'dp'), may hold values from -0.0625 to 0.0625
- student_down: bfloat16 [8, 1792, 8192], P('expert', 'neuron', 'dp'), may hold values from -0.125 to 0.125
- routes: int32 [512, 2], replicated, may hold values from 0 to 7, all different within a row; in each aligned block of 8 rows (0 to 7, 8 to 15, ...) at most 6 rows name the same one
- route_weight: float32 [512, 2], replicated, may hold values from 0.25 to 1
Outputs:
- grad_gate: bfloat16 [8, 1792, 8192], P('expert', 'neuron', 'dp')
- grad_up: bfloat16 [8, 1792, 8192], P('expert', 'neuron', 'dp')
- grad_down: bfloat16 [8, 1792, 8192], P('expert', 'neuron', 'dp')
The draws below stay inside these ranges and needn't reach their ends.
Inputs may be any that keep to these rules, and one draw needn't show every extreme that they name: `routes`: each token names 2 different experts. In each aligned block of 8 tokens (the tokens of one index of neuron and expert) no expert is named by more than 6 tokens, a bound that some block reaches.
All inputs are finite; a program needn't handle non-finite values.
Results may differ from the reference program's by a relative error of at most 0.008.
Values may be sent and summed in bfloat16 or wider, within the bound.
A program may use at most 128 MiB of HBM per device.

```python
import math
import jax
import jax.numpy as jnp
import numpy as np
from jax import lax

D = 8192
FF = 28672
E = 8
H = 1792
TOP = 2
ROWS = 8
TOKENS = 512
MOST = 6
CAP = 384


def shard_levels(stream_key, shape, split, low, largest):
    gain = 1.0
    for axis_at, shards_of in split:
        steps = jax.random.uniform(jax.random.fold_in(jax.random.fold_in(stream_key, 6), axis_at), (shards_of,), jnp.float32, low / len(split), largest / len(split))
        gain = gain * jnp.repeat(jnp.exp(steps), shape[axis_at] // shards_of).reshape((-1,) + (1,) * (len(shape) - 1 - axis_at))
    return gain


def assign_block(key, own, number, rows, amount, top, most, skew):
    ranking = jax.random.permutation(key, amount)
    crowded, ordinary = portions_of(amount, rows * top, most, skew, True), portions_of(amount, rows * top, most, skew, False)
    places = jnp.arange(amount)

    def named(tallies, rotation):
        used = int((tallies > 0).sum())
        fixed = max(1, used // 4)
        passed = fixed + (places - fixed + rotation * (used - fixed)) % max(1, amount - fixed)
        return jnp.zeros((amount,), jnp.int32).at[ranking[jnp.where(places < fixed, places, passed)]].set(jnp.asarray(tallies, jnp.int32))

    tallies = jnp.where(number % 4 == 0, named(crowded, number // 4), named(ordinary, number - number // 4 - 1))
    mixed = jax.random.permutation(jax.random.fold_in(own, 3), amount)
    donor, sink = mixed[0:amount // 2 * 2:2], mixed[1:amount // 2 * 2:2]
    slack = jnp.minimum(tallies[donor] - 1, most - tallies[sink]) // 2
    slack = jnp.where((donor == ranking[0]) | (sink == ranking[0]) | (tallies[sink] == 0), 0, jnp.maximum(slack, 0))
    passed = jax.random.randint(jax.random.fold_in(own, 4), (amount // 2,), 0, 1 << 20) % (slack + 1)
    tallies = tallies.at[donor].add(-passed).at[sink].add(passed)
    labels = jnp.searchsorted(jnp.cumsum(tallies), jnp.arange(rows * top), side="right").astype(jnp.int32)
    listing = labels.reshape(top, rows).T
    listing = listing[jax.random.permutation(jax.random.fold_in(own, 1), rows)]
    rotation = jax.random.randint(jax.random.fold_in(own, 2), (rows, 1), 0, top)
    return jnp.take_along_axis(listing, (jnp.arange(top)[None, :] + rotation) % top, axis=1)


def portions_of(count, total, bound, skew, full):
    loads = [(1 << 20) // math.isqrt(grade ** skew) + 1 for grade in range(1, count + 1)]
    largest = bound if full else min(bound, max(-(-total // count), total * loads[0] // sum(loads)))
    least = 1 if total - largest >= count - 1 else 0
    holding, surplus = [largest] + [least] * (count - 1), total - largest - least * (count - 1)
    while surplus > 0:
        movable = [i for i in range(1, count) if holding[i] < largest] or [i for i in range(1, count) if holding[i] < bound]
        mass, budget = sum([loads[i] for i in movable]), surplus
        for i in movable:
            addition = min(bound - holding[i], max(1, budget * loads[i] // mass), surplus)
            holding[i] = holding[i] + addition
            surplus = surplus - addition
    return np.array(holding)


def gaussian(own_key, dims, deviation, bound, shards=(), kind=jnp.bfloat16):
    entries = jax.random.normal(own_key, dims, jnp.float32) * deviation
    if len(shards) > 0:
        entries = shard_levels(own_key, dims, shards, -0.22, 0.18) * entries
    return jnp.clip(entries, min=-bound, max=bound).astype(kind)


def setup_inputs(seed: int = 0) -> dict:
    seeds = jax.random.split(jax.random.key(seed), 10)
    tokens = gaussian(seeds[0], (TOKENS, D), 1.0, 6.0, ((0, 64), (1, 4)))
    teacher_gate = gaussian(seeds[1], (FF, D), D ** -0.5, 0.0625, ((0, 64), (1, 4)))
    teacher_up = gaussian(seeds[2], (FF, D), D ** -0.5, 0.0625, ((0, 64), (1, 4)))
    teacher_down = gaussian(seeds[3], (FF, D), FF ** -0.5, 0.03125, ((0, 64), (1, 4)))
    student_gate = gaussian(seeds[4], (E, H, D), D ** -0.5, 0.0625, ((0, 8), (1, 8), (2, 4)))
    student_up = gaussian(seeds[5], (E, H, D), D ** -0.5, 0.0625, ((0, 8), (1, 8), (2, 4)))
    student_down = gaussian(seeds[6], (E, H, D), H ** -0.5, 0.125, ((0, 8), (1, 8), (2, 4)))
    routes_keys = jax.random.split(jax.random.fold_in(seeds[7], 1), TOKENS // ROWS)
    routes_turns = jax.random.permutation(jax.random.fold_in(seeds[7], 3), TOKENS // ROWS)
    routes = jax.vmap(lambda own, number: assign_block(jax.random.fold_in(seeds[7], 2), own, number, ROWS, E, TOP, MOST, 2))(routes_keys, routes_turns).reshape((TOKENS, TOP))
    route_weight = jnp.clip(jax.random.uniform(seeds[8], (TOKENS, TOP), jnp.float32, 0.25, 1.0), 0.25, 1.0)
    return dict(tokens=tokens, teacher_gate=teacher_gate, teacher_up=teacher_up, teacher_down=teacher_down, student_gate=student_gate, student_up=student_up, student_down=student_down, routes=routes, route_weight=route_weight)


def silu_parts(pre_values):
    sigmoid_part = jax.nn.sigmoid(pre_values)
    return sigmoid_part, pre_values * sigmoid_part


def reference(tokens, teacher_gate, teacher_up, teacher_down, student_gate, student_up, student_down, routes, route_weight):
    contract = (((1,), (1,)), ((), ()))
    over_rows = (((0,), (0,)), ((), ()))
    teacher_pre = lax.dot_general(tokens, teacher_gate, contract, preferred_element_type=jnp.float32)
    teacher_lift = lax.dot_general(tokens, teacher_up, contract, preferred_element_type=jnp.float32)
    teacher_hidden = (jax.nn.silu(teacher_pre) * teacher_lift).astype(jnp.bfloat16)
    target = jnp.dot(teacher_hidden, teacher_down, preferred_element_type=jnp.float32)
    student = jnp.zeros((TOKENS, D), jnp.float32)
    saved = []
    for expert in range(E):
        chosen = routes == expert
        picked = jnp.any(chosen, axis=1)
        mixing = jnp.sum(jnp.where(chosen, route_weight, jnp.zeros_like(route_weight)), axis=1)
        positions = jnp.nonzero(picked, size=CAP, fill_value=0)[0].astype(jnp.int32)
        valid = jnp.arange(CAP, dtype=jnp.int32) < jnp.sum(picked.astype(jnp.int32))
        slot_tokens = jnp.where(valid[:, None], tokens[positions], jnp.zeros((), tokens.dtype))
        slot_mixing = jnp.where(valid, mixing[positions], jnp.zeros((), mixing.dtype))
        expert_pre = lax.dot_general(slot_tokens, student_gate[expert], contract, preferred_element_type=jnp.float32)
        expert_lift = lax.dot_general(slot_tokens, student_up[expert], contract, preferred_element_type=jnp.float32)
        sigmoid_part, activated = silu_parts(expert_pre)
        expert_hidden = (activated * expert_lift).astype(jnp.bfloat16)
        output = jnp.dot(expert_hidden, student_down[expert], preferred_element_type=jnp.float32)
        student = student.at[positions].add(slot_mixing[:, None] * output)
        saved.append((positions, slot_tokens, slot_mixing, expert_pre, expert_lift, sigmoid_part, activated, expert_hidden))
    residual = (student - target).astype(jnp.bfloat16)
    grads_gate = []
    grads_up = []
    grads_down = []
    for expert in range(E):
        positions, slot_tokens, slot_mixing, expert_pre, expert_lift, sigmoid_part, activated, expert_hidden = saved[expert]
        slot_grad = (slot_mixing[:, None] * residual[positions].astype(jnp.float32)).astype(jnp.bfloat16)
        grads_down.append(lax.dot_general(expert_hidden, slot_grad, over_rows, preferred_element_type=jnp.float32).astype(jnp.bfloat16))
        hidden_grad = lax.dot_general(slot_grad, student_down[expert], contract, preferred_element_type=jnp.float32)
        slope = sigmoid_part * (1.0 + expert_pre * (1.0 - sigmoid_part))
        pre_grad = (hidden_grad * expert_lift * slope).astype(jnp.bfloat16)
        lift_grad = (hidden_grad * activated).astype(jnp.bfloat16)
        grads_gate.append(lax.dot_general(pre_grad, slot_tokens, over_rows, preferred_element_type=jnp.float32).astype(jnp.bfloat16))
        grads_up.append(lax.dot_general(lift_grad, slot_tokens, over_rows, preferred_element_type=jnp.float32).astype(jnp.bfloat16))
    return jnp.stack(grads_gate), jnp.stack(grads_up), jnp.stack(grads_down)
```

```python
import jax
import jax.numpy as jnp
from jax import lax
from jax.experimental import pallas as pl
from jax.experimental.pallas import tpu as pltpu
from jax.sharding import PartitionSpec as P

MESH = pl.DeviceIdType.MESH
F32, BF16 = jnp.float32, jnp.bfloat16
NX, NY, NZ = 4, 4, 8
ROWS = 16
WIDTH, HALF = 2048, 1024
TEACH, STUD = 448, 224
TQ, SQ = 112, 64
HQ = TQ + SQ
CHUNK = 256
ORDER = (0, 1, 7, 2, 6, 3, 5, 4)
POS = tuple(ORDER.index(k) for k in range(NZ))
PC = 256
ZSEND = (7, 1, 6, 2, 5, 3, 4)
NSEM = 160
NT = (((1,), (1,)), ((), ()))


def dot(a, b, dims=(((1,), (0,)), ((), ()))):
    return lax.dot_general(a, b, dims, preferred_element_type=F32)


def kernel(
    tokens, mix, tgate, tup, tdown, sgate, sup, sdown,
    ggate, gup, gdown,
    w1, wd, tok, res, tf, blk, psend, prec, pown, hall, spre, slift,
    fcore, rcore, facc, fsend, rz, ry, qsend, rqz, ysend, rpy,
    isend, irec, iown, grads, lsem, ssem, rsem,
):
    ix, iz, ie = lax.axis_index("dp"), lax.axis_index("neuron"), lax.axis_index("expert")
    iy, ic = ie // 2, lax.rem(ie, 2)
    oc = 1 - ic

    def dev(x=0, y=0, z=0, c=0):
        core = oc if c else ic
        return (lax.rem(ix + x, NX), lax.rem(iz + z, NZ), lax.rem(iy + y, NY) * 2 + core)

    partners = (
        [dev(x=k) for k in range(1, NX)] + [dev(y=k) for k in range(1, NY)]
        + [dev(z=k) for k in range(1, NZ)] + [dev(c=1)]
    )
    barrier = pltpu.get_barrier_semaphore()
    for p in partners:
        pl.semaphore_signal(barrier, inc=1, device_id=p, device_id_type=MESH)

    loads = []

    def load(src, dst):
        cp = pltpu.make_async_copy(src, dst, lsem.at[len(loads)])
        cp.start()
        loads.append(cp)

    zero = jnp.zeros((SQ // 2, WIDTH), BF16)
    w1[3, TQ + 32:HQ] = zero
    w1[3, HQ + TQ + 32:] = zero
    for h in range(2):
        wd[h, 3, TQ + 32:HQ] = jnp.zeros((SQ // 2, HALF), BF16)
    for j in range(NX):
        n = SQ if j < 3 else SQ // 2
        load(tgate.at[pl.ds(j * TQ, TQ)], w1.at[j, pl.ds(0, TQ)])
        load(sgate.at[0, pl.ds(j * SQ, n)], w1.at[j, pl.ds(TQ, n)])
        load(tup.at[pl.ds(j * TQ, TQ)], w1.at[j, pl.ds(HQ, TQ)])
        load(sup.at[0, pl.ds(j * SQ, n)], w1.at[j, pl.ds(HQ + TQ, n)])
    n_w1 = len(loads)
    for j in range(NX):
        n = SQ if j < 3 else SQ // 2
        for h in range(2):
            cols = pl.ds(h * HALF, HALF)
            load(tdown.at[pl.ds(j * TQ, TQ), cols], wd.at[h, j, pl.ds(0, TQ)])
            load(sdown.at[0, pl.ds(j * SQ, n), cols], wd.at[h, j, pl.ds(TQ, n)])

    for h in range(2):
        tf[h] = tokens[:, h * HALF:(h + 1) * HALF].astype(F32)
    blk[pl.ds(pl.multiple_of(ic * 8, 8), 8), :] = tf[ic]
    pl.semaphore_wait(barrier, len(partners))

    sent = []

    def send(src, dst, to):
        i = len(sent)
        cp = pltpu.make_async_remote_copy(
            src_ref=src, dst_ref=dst, send_sem=ssem.at[i], recv_sem=rsem.at[i],
            device_id=to, device_id_type=MESH,
        )
        cp.start()
        sent.append(cp)
        return cp

    cp = send(tf.at[oc], blk.at[pl.ds(pl.multiple_of(ic * 8, 8), 8), :], dev(c=1))
    cp.wait_recv()
    tok[ic, 0, 0:ROWS] = blk[...].astype(BF16)

    pcols, qcols = pl.ds(0, PC), pl.ds(PC, HALF - PC)

    def rows(k):
        return pl.ds((k % NY) * ROWS, ROWS)

    def gather_start(buf):
        own = buf.at[ic, 0, pl.ds(0, ROWS)]
        p1 = [send(own.at[:, pcols], buf.at[ic, 0, rows(-k), pcols], dev(y=k)) for k in (2, 1, 3)]
        q1 = {k: send(own.at[:, qcols], buf.at[ic, POS[-k % NZ], pl.ds(0, ROWS), qcols], dev(z=k))
              for k in ZSEND}
        for c in p1:
            c.wait_recv()
        p2 = {k: send(buf.at[ic, 0, :, pcols], buf.at[ic, POS[-k % NZ], :, pcols], dev(z=k))
              for k in ZSEND}
        return q1, p2

    def gather_spread(buf, q1, half):
        for k in (ZSEND[:3] if half == 0 else ZSEND[3:]):
            q1[k].wait_recv()
        group = pl.ds(half * 4, 4)
        return [send(buf.at[ic, group, pl.ds(0, ROWS), qcols], buf.at[ic, group, rows(-k), qcols], dev(y=k))
                for k in (2, 1, 3)]

    def gather_core(buf, p2, q2, half):
        for k in (ZSEND[:3] if half == 0 else ZSEND[3:]):
            p2[k].wait_recv()
        for c in q2:
            c.wait_recv()
        group = pl.ds(half * 4, 4)
        return send(buf.at[ic, group], buf.at[ic, group], dev(c=1))

    q1, p2 = gather_start(tok)
    q2a = gather_spread(tok, q1, 0)
    core_a = gather_core(tok, p2, q2a, 0)
    q2b = gather_spread(tok, q1, 1)
    for cp in loads[:n_w1]:
        cp.wait()
    core_a.wait_recv()

    def piece(buf, h, half):
        return buf[h, half * 4:half * 4 + 4].reshape(CHUNK, HALF)

    def hidden_parts(half):
        out = []
        for d in (2, 1, 3, 0):
            j = lax.rem(ix + d, NX)
            part = dot(w1[j, :, :HALF], piece(tok, 0, half), NT) + dot(w1[j, :, HALF:], piece(tok, 1, half), NT)
            if d == 0:
                pown[half] = part
            else:
                psend[half, d] = part.astype(BF16)
                out.append(send(psend.at[half, d], prec.at[half, NX - d], dev(x=d)))
        return out

    def activate(half, cps):
        for c in cps:
            c.wait_recv()
        total = pown[half]
        for d in range(1, NX):
            total = total + prec[half, d].astype(F32)
        pre, lift = total[:HQ], total[HQ:]
        cols = pl.ds(half * CHUNK, CHUNK)
        spre[:, cols] = pre[TQ:]
        slift[:, cols] = lift[TQ:]
        act = pre * jax.nn.sigmoid(pre) * lift
        hall[half, ix, 0:TQ] = (-act[:TQ]).astype(BF16)
        hall[half, ix, TQ:HQ] = (act[TQ:] * mix[:, cols]).astype(BF16)
        mine = hall.at[half, ix]
        return [send(mine, mine, dev(x=d)) for d in (2, 1, 3)]

    def outputs(half, cps):
        for c in cps:
            c.wait_recv()
        hidden = hall[half].reshape(NX * HQ, CHUNK).T
        fcore[half] = dot(hidden, wd[oc].reshape(NX * HQ, HALF)).astype(BF16)
        cp = send(fcore.at[half], rcore.at[half], dev(c=1))
        facc[half] = dot(hidden, wd[ic].reshape(NX * HQ, HALF))
        return cp

    def scatter_first(half, cp):
        cp.wait_recv()
        total = facc[half] + rcore[half].astype(F32)
        facc[half] = total
        fsend[half * 4:half * 4 + 4] = total.astype(BF16).reshape(4, 64, HALF)
        q = [send(fsend.at[pl.ds(half * 4, 4), rows(k), qcols], ry.at[half, NY - k], dev(y=k)) for k in (2, 1, 3)]
        p = []
        for pos in range(half * 4, half * 4 + 4):
            k = ORDER[pos]
            if k:
                p.append(send(fsend.at[pos, :, pcols], rz.at[POS[-k % NZ]], dev(z=k)))
        return q, p

    def scatter_second(half, q):
        for c in q:
            c.wait_recv()
        total = facc[half].reshape(4, 64, HALF)[:, :ROWS, PC:]
        for d in range(1, NY):
            total = total + ry[half, d].astype(F32)
        if half == 0:
            ysend[0:ROWS, PC:] = total[0]
        qsend[half * 4:half * 4 + 4] = total.astype(BF16)
        out = []
        for pos in range(half * 4, half * 4 + 4):
            k = ORDER[pos]
            if k:
                out.append(send(qsend.at[pos], rqz.at[POS[-k % NZ]], dev(z=k)))
        return out

    c0 = hidden_parts(0)
    core_b = gather_core(tok, p2, q2b, 1)
    core_b.wait_recv()
    c1 = hidden_parts(1)
    d0 = activate(0, c0)
    for cp in loads[n_w1:]:
        cp.wait()
    e0 = outputs(0, d0)
    f0q, f0p = scatter_first(0, e0)
    d1 = activate(1, c1)
    g0 = scatter_second(0, f0q)
    e1 = outputs(1, d1)
    f1q, f1p = scatter_first(1, e1)
    g1 = scatter_second(1, f1q)

    for c in f0p + f1p:
        c.wait_recv()
    total = facc[0, 0:64, :PC]
    for pos in range(1, NZ):
        total = total + rz[pos].astype(F32)
    ysend[:, :PC] = total
    qy = rpy.at[0]
    qy[...] = total.astype(BF16)
    hs = [send(rpy.at[0, rows(k)], rpy.at[NY - k, pl.ds(0, ROWS)], dev(y=k)) for k in (2, 1, 3)]
    for c in g0 + g1:
        c.wait_recv()
    total = ysend[0:ROWS, PC:]
    for pos in range(1, NZ):
        total = total + rqz[pos].astype(F32)
    res[ic, 0, 0:ROWS, PC:] = total.astype(BF16)
    for c in hs:
        c.wait_recv()
    total = ysend[0:ROWS, :PC]
    for d in range(1, NY):
        total = total + rpy[d, 0:ROWS].astype(F32)
    res[ic, 0, 0:ROWS, :PC] = total.astype(BF16)

    q1, p2 = gather_start(res)
    q2a = gather_spread(res, q1, 0)
    core_a = gather_core(res, p2, q2a, 0)
    q2b = gather_spread(res, q1, 1)
    core_a.wait_recv()

    def hidden_grads(half):
        out = []
        for d in (2, 1, 3, 0):
            j = lax.rem(ix + d, NX)
            part = dot(wd[0, j, TQ:], piece(res, 0, half), NT) + dot(wd[1, j, TQ:], piece(res, 1, half), NT)
            if d == 0:
                iown[half] = part
            else:
                isend[half, d] = part.astype(BF16)
                out.append(send(isend.at[half, d], irec.at[half, NX - d], dev(x=d)))
        return out

    def slopes(half, cps):
        for c in cps:
            c.wait_recv()
        total = iown[half]
        for d in range(1, NX):
            total = total + irec[half, d].astype(F32)
        cols = pl.ds(half * CHUNK, CHUNK)
        total = total * mix[:, cols]
        pre, lift = spre[:, cols], slift[:, cols]
        s = jax.nn.sigmoid(pre)
        grads[half, 0, ix] = (total * lift * (s * (1.0 + pre * (1.0 - s)))).astype(BF16)
        grads[half, 1, ix] = (total * (pre * s)).astype(BF16)
        mine = grads.at[half, :, ix]
        return [send(mine, mine, dev(x=d)) for d in (2, 1, 3)]

    i0 = hidden_grads(0)
    core_b = gather_core(res, p2, q2b, 1)
    core_b.wait_recv()
    i1 = hidden_grads(1)
    j0 = slopes(0, i0)

    def product(left, buf, h):
        return dot(left[0], piece(buf, h, 0)) + dot(left[1], piece(buf, h, 1))

    hm = [hall[half, :, TQ:].reshape(NX * SQ, CHUNK) for half in range(2)]
    for h in range(2):
        gdown[0, :, h * HALF:(h + 1) * HALF] = product(hm, res, h)[:STUD].astype(BF16)
    j1 = slopes(1, i1)
    for c in j0 + j1:
        c.wait_recv()
    for n, out in enumerate((ggate, gup)):
        left = [grads[half, n].reshape(NX * SQ, CHUNK) for half in range(2)]
        for h in range(2):
            out[0, :, h * HALF:(h + 1) * HALF] = product(left, tok, h)[:STUD].astype(BF16)
    for c in sent:
        c.wait_send()


def body(tokens, tgate, tup, tdown, sgate, sup, sdown, routes, route_weight):
    iz, ie = lax.axis_index("neuron"), lax.axis_index("expert")
    mixing = jnp.sum(jnp.where(routes == ie, route_weight, 0.0), axis=1).reshape(NZ, NY, ROWS)
    zs = lax.rem(iz + jnp.array(ORDER, jnp.int32), NZ)
    ys = lax.rem(ie // 2 + jnp.arange(NY, dtype=jnp.int32), NY)
    mix = mixing[zs][:, ys].reshape(1, NZ * NY * ROWS)
    vmem, anym = pl.BlockSpec(memory_space=pltpu.VMEM), pl.BlockSpec(memory_space=pl.ANY)
    grad = jax.ShapeDtypeStruct((1, STUD, WIDTH), BF16)
    V = pltpu.VMEM
    return pl.pallas_call(
        kernel,
        out_shape=(grad, grad, grad),
        in_specs=[vmem, vmem] + [anym] * 6,
        out_specs=(vmem, vmem, vmem),
        scratch_shapes=[
            V((NX, 2 * HQ, WIDTH), BF16),
            V((2, NX, HQ, HALF), BF16),
            V((2, NZ, 64, HALF), BF16),
            V((2, NZ, 64, HALF), BF16),
            V((2, 8, HALF), F32),
            V((ROWS, HALF), F32),
            V((2, NX, 2 * HQ, CHUNK), BF16),
            V((2, NX, 2 * HQ, CHUNK), BF16),
            V((2, 2 * HQ, CHUNK), F32),
            V((2, NX, HQ, CHUNK), BF16),
            V((SQ, 2 * CHUNK), F32),
            V((SQ, 2 * CHUNK), F32),
            V((2, CHUNK, HALF), BF16),
            V((2, CHUNK, HALF), BF16),
            V((2, CHUNK, HALF), F32),
            V((NZ, 64, HALF), BF16),
            V((NZ, 64, PC), BF16),
            V((2, NY, 4, ROWS, HALF - PC), BF16),
            V((NZ, ROWS, HALF - PC), BF16),
            V((NZ, ROWS, HALF - PC), BF16),
            V((64, HALF), F32),
            V((NY, 64, PC), BF16),
            V((2, NX, SQ, CHUNK), BF16),
            V((2, NX, SQ, CHUNK), BF16),
            V((2, SQ, CHUNK), F32),
            V((2, 2, NX, SQ, CHUNK), BF16),
            pltpu.SemaphoreType.DMA((32,)),
            pltpu.SemaphoreType.DMA((NSEM,)),
            pltpu.SemaphoreType.DMA((NSEM,)),
        ],
        compiler_params=pltpu.CompilerParams(
            collective_id=0, has_side_effects=True, vmem_limit_bytes=56 * 2**20
        ),
        cost_estimate=pl.CostEstimate(flops=6 * 10**9, bytes_accessed=12 * 10**6, transcendentals=10**6),
        name="distill",
    )(tokens, mix, tgate, tup, tdown, sgate, sup, sdown)


def solution(mesh):
    split = P(("neuron", "expert"), "dp")
    expert = P("expert", "neuron", "dp")
    return jax.shard_map(
        body,
        mesh=mesh,
        in_specs=(split, split, split, split, expert, expert, expert, P(), P()),
        out_specs=(expert, expert, expert),
        check_vma=False,
    )
```

```python
import jax
import jax.numpy as jnp
from jax import lax
from jax.experimental import pallas as pl
from jax.experimental.pallas import tpu as pltpu
from jax.sharding import PartitionSpec as P

MESH = pl.DeviceIdType.MESH
F32, BF16 = jnp.float32, jnp.bfloat16
NX, NY, NZ = 4, 4, 8
ROWS = 16
WIDTH, HALF = 2048, 1024
TEACH, STUD = 448, 224
TQ, SQ = 112, 64
HQ = TQ + SQ
CHUNK, PARTS, SLABS = 128, 4, 2
TOKENS = CHUNK * PARTS
ORDER = (0, 1, 7, 2, 6, 3, 5, 4)
POS = tuple(ORDER.index(k) for k in range(NZ))
PC = 256
ZSEND = ((7,), (1, 6), (2, 5), (3, 4))
NSEM = 176
NT = (((1,), (1,)), ((), ()))


def dot(a, b, dims=(((1,), (0,)), ((), ()))):
    return lax.dot_general(a, b, dims, preferred_element_type=F32)


def kernel(
    tokens, routes, weights, tgate, tup, tdown, sgate, sup, sdown,
    tok, res, pgrad, lgrad, hm,
    w1, wd, tf, blk, mix, psend, prec, pown, hall, fac,
    fcore, rcore, facc, fsend, rz, ry, qsend, rqz, ysend, rpy,
    isend, irec, iown, hgrad, lsem, ssem, rsem,
):
    ix, iz, ie = lax.axis_index("dp"), lax.axis_index("neuron"), lax.axis_index("expert")
    iy, ic = ie // 2, lax.rem(ie, 2)
    oc = 1 - ic

    def dev(x=0, y=0, z=0, c=0):
        core = oc if c else ic
        return (lax.rem(ix + x, NX), lax.rem(iz + z, NZ), lax.rem(iy + y, NY) * 2 + core)

    partners = (
        [dev(x=k) for k in range(1, NX)] + [dev(y=k) for k in range(1, NY)]
        + [dev(z=k) for k in range(1, NZ)] + [dev(c=1)]
    )
    barrier = pltpu.get_barrier_semaphore()
    for p in partners:
        pl.semaphore_signal(barrier, inc=1, device_id=p, device_id_type=MESH)

    loads = []

    def load(src, dst):
        cp = pltpu.make_async_copy(src, dst, lsem.at[len(loads)])
        cp.start()
        loads.append(cp)

    zero = jnp.zeros((SQ // 2, WIDTH), BF16)
    w1[3, TQ + 32:HQ] = zero
    w1[3, HQ + TQ + 32:] = zero
    for h in range(2):
        wd[h, 3, TQ + 32:HQ] = jnp.zeros((SQ // 2, HALF), BF16)
    for j in range(NX):
        n = SQ if j < 3 else SQ // 2
        load(tgate.at[pl.ds(j * TQ, TQ)], w1.at[j, pl.ds(0, TQ)])
        load(sgate.at[0, pl.ds(j * SQ, n)], w1.at[j, pl.ds(TQ, n)])
        load(tup.at[pl.ds(j * TQ, TQ)], w1.at[j, pl.ds(HQ, TQ)])
        load(sup.at[0, pl.ds(j * SQ, n)], w1.at[j, pl.ds(HQ + TQ, n)])
    n_w1 = len(loads)
    for j in range(NX):
        n = SQ if j < 3 else SQ // 2
        for h in range(2):
            cols = pl.ds(h * HALF, HALF)
            load(tdown.at[pl.ds(j * TQ, TQ), cols], wd.at[h, j, pl.ds(0, TQ)])
            load(sdown.at[0, pl.ds(j * SQ, n), cols], wd.at[h, j, pl.ds(TQ, n)])

    for h in range(2):
        tf[h] = tokens[:, h * HALF:(h + 1) * HALF].astype(F32)
    blk[pl.ds(pl.multiple_of(ic * 8, 8), 8), :] = tf[ic]
    pl.semaphore_wait(barrier, len(partners))

    sent = []

    def send(src, dst, to):
        i = len(sent)
        cp = pltpu.make_async_remote_copy(
            src_ref=src, dst_ref=dst, send_sem=ssem.at[i], recv_sem=rsem.at[i],
            device_id=to, device_id_type=MESH,
        )
        cp.start()
        sent.append(cp)
        return cp

    def arrived(cps):
        for c in cps:
            c.wait_recv()

    cp = send(tf.at[oc], blk.at[pl.ds(pl.multiple_of(ic * 8, 8), 8), :], dev(c=1))
    cp.wait_recv()
    tok[ic, 0, 0:ROWS] = blk[...].astype(BF16)

    pcols, qcols = pl.ds(0, PC), pl.ds(PC, HALF - PC)

    def rows(k):
        return pl.ds((k % NY) * ROWS, ROWS)

    def group(part):
        return pl.ds(part * SLABS, SLABS)

    def gather_start(buf):
        own = buf.at[ic, 0, pl.ds(0, ROWS)]
        p1 = [send(own.at[:, pcols], buf.at[ic, 0, rows(-k), pcols], dev(y=k)) for k in (2, 1, 3)]
        q1 = [[send(own.at[:, qcols], buf.at[ic, POS[-k % NZ], pl.ds(0, ROWS), qcols], dev(z=k)) for k in ks]
              for ks in ZSEND]
        arrived(p1)
        p2 = [[send(buf.at[ic, 0, :, pcols], buf.at[ic, POS[-k % NZ], :, pcols], dev(z=k)) for k in ks]
              for ks in ZSEND]
        return [q1, p2, [None] * PARTS, [None] * PARTS]

    def spread(buf, state, part):
        arrived(state[0][part])
        g = group(part)
        state[2][part] = [
            send(buf.at[ic, g, pl.ds(0, ROWS), qcols], buf.at[ic, g, rows(-k), qcols], dev(y=k)) for k in (2, 1, 3)
        ]

    def to_core(buf, state, part):
        arrived(state[1][part])
        arrived(state[2][part])
        state[3][part] = send(buf.at[ic, group(part)], buf.at[ic, group(part)], dev(c=1))

    def piece(buf, h, part):
        return buf[h, part * SLABS:(part + 1) * SLABS].reshape(CHUNK, HALF)

    def hidden_parts(part):
        out = []
        for d in (2, 1, 3, 0):
            j = lax.rem(ix + d, NX)
            val = dot(w1[j, :, :HALF], piece(tok, 0, part), NT) + dot(w1[j, :, HALF:], piece(tok, 1, part), NT)
            if d == 0:
                pown[part] = val
            else:
                psend[part, d] = val.astype(BF16)
                out.append(send(psend.at[part, d], prec.at[part, NX - d], dev(x=d)))
        return out

    def activate(part, cps):
        arrived(cps)
        total = pown[part]
        for d in range(1, NX):
            total = total + prec[part, d].astype(F32)
        pre, lift = total[:HQ], total[HQ:]
        s = jax.nn.sigmoid(pre)
        act = pre * s
        hidden = act * lift
        weight = mix[part, 0:1]
        hall[part, ix, 0:TQ] = (-hidden[:TQ]).astype(BF16)
        hall[part, ix, TQ:HQ] = (hidden[TQ:] * weight).astype(BF16)
        mine = hall.at[part, ix]
        out = [send(mine, mine, dev(x=d)) for d in (2, 1, 3)]
        slope = s * (1.0 + pre * (1.0 - s))
        fac[ix, part, 0] = (weight * (lift * slope)[TQ:]).astype(BF16)
        fac[ix, part, 1] = (weight * act[TQ:]).astype(BF16)
        return out

    def outputs(part, cps):
        arrived(cps)
        hidden = hall[part].reshape(NX * HQ, CHUNK).T
        fcore[part] = dot(hidden, wd[oc].reshape(NX * HQ, HALF)).astype(BF16)
        cp = send(fcore.at[part], rcore.at[part], dev(c=1))
        facc[part] = dot(hidden, wd[ic].reshape(NX * HQ, HALF))
        return cp

    def scatter_first(part, cp):
        cp.wait_recv()
        total = facc[part] + rcore[part].astype(F32)
        facc[part] = total
        fsend[part * SLABS:(part + 1) * SLABS] = total.astype(BF16).reshape(SLABS, 64, HALF)
        q = [send(fsend.at[group(part), rows(k), qcols], ry.at[part, NY - k], dev(y=k)) for k in (2, 1, 3)]
        p = []
        for pos in range(part * SLABS, (part + 1) * SLABS):
            k = ORDER[pos]
            if k:
                p.append(send(fsend.at[pos, :, pcols], rz.at[POS[-k % NZ]], dev(z=k)))
        return q, p

    def scatter_second(part, q):
        arrived(q)
        total = facc[part].reshape(SLABS, 64, HALF)[:, :ROWS, PC:]
        for d in range(1, NY):
            total = total + ry[part, d].astype(F32)
        if part == 0:
            ysend[0:ROWS, PC:] = total[0]
        qsend[part * SLABS:(part + 1) * SLABS] = total.astype(BF16)
        out = []
        for pos in range(part * SLABS, (part + 1) * SLABS):
            k = ORDER[pos]
            if k:
                out.append(send(qsend.at[pos], rqz.at[POS[-k % NZ]], dev(z=k)))
        return out

    def mixing():
        m = jnp.sum(jnp.where(routes[...] == ie, weights[...], 0.0), axis=0, keepdims=True)
        m = jnp.broadcast_to(m, (8, TOKENS))
        m = pltpu.roll(m, lax.rem(NZ - iz, NZ) * 64, 1)
        lane = lax.broadcasted_iota(jnp.int32, (8, TOKENS), 1)
        near = pltpu.roll(m, lax.rem(TOKENS - iy * ROWS, TOKENS), 1)
        far = pltpu.roll(m, 64 - iy * ROWS, 1)
        m = jnp.where(lax.rem(lane, 64) < 64 - iy * ROWS, near, far)
        low = lax.broadcasted_iota(jnp.int32, (8, CHUNK), 1) < 64
        for part in range(PARTS):
            two = []
            for side in range(2):
                k = ORDER[part * 2 + side]
                t = m[:, (k // 2) * CHUNK:(k // 2 + 1) * CHUNK]
                two.append(t if k % 2 == side else pltpu.roll(t, 64, 1))
            mix[part] = jnp.where(low, two[0], two[1])

    P4 = range(PARTS)
    c, d, e, q, p, g = ([None] * PARTS for _ in range(6))
    state = gather_start(tok)
    mixing()
    spread(tok, state, 0)
    spread(tok, state, 1)
    to_core(tok, state, 0)
    spread(tok, state, 2)
    for cp in loads[:n_w1]:
        cp.wait()
    state[3][0].wait_recv()
    c[0] = hidden_parts(0)
    to_core(tok, state, 1)
    spread(tok, state, 3)
    state[3][1].wait_recv()
    c[1] = hidden_parts(1)
    to_core(tok, state, 2)
    state[3][2].wait_recv()
    c[2] = hidden_parts(2)
    to_core(tok, state, 3)
    d[0] = activate(0, c[0])
    state[3][3].wait_recv()
    c[3] = hidden_parts(3)
    d[1] = activate(1, c[1])
    for cp in loads[n_w1:]:
        cp.wait()
    e[0] = outputs(0, d[0])
    d[2] = activate(2, c[2])
    q[0], p[0] = scatter_first(0, e[0])
    e[1] = outputs(1, d[1])
    d[3] = activate(3, c[3])
    factors = [send(fac.at[ix], fac.at[ix], dev(x=k)) for k in (2, 1, 3)]
    g[0] = scatter_second(0, q[0])
    q[1], p[1] = scatter_first(1, e[1])
    e[2] = outputs(2, d[2])
    g[1] = scatter_second(1, q[1])
    q[2], p[2] = scatter_first(2, e[2])
    e[3] = outputs(3, d[3])
    g[2] = scatter_second(2, q[2])
    q[3], p[3] = scatter_first(3, e[3])
    g[3] = scatter_second(3, q[3])

    total = facc[0, 0:64, :PC]
    for part in P4:
        arrived(p[part])
    for pos in range(1, NZ):
        total = total + rz[pos].astype(F32)
    ysend[:, :PC] = total
    rpy[0] = total.astype(BF16)
    hs = [send(rpy.at[0, rows(k)], rpy.at[NY - k, pl.ds(0, ROWS)], dev(y=k)) for k in (2, 1, 3)]
    for part in P4:
        arrived(g[part])
    total = ysend[0:ROWS, PC:]
    for pos in range(1, NZ):
        total = total + rqz[pos].astype(F32)
    res[ic, 0, 0:ROWS, PC:] = total.astype(BF16)
    arrived(hs)
    total = ysend[0:ROWS, :PC]
    for k in range(1, NY):
        total = total + rpy[k, 0:ROWS].astype(F32)
    res[ic, 0, 0:ROWS, :PC] = total.astype(BF16)

    def hidden_grads(part):
        out = []
        for d in (2, 1, 3, 0):
            j = lax.rem(ix + d, NX)
            val = dot(wd[0, j, TQ:], piece(res, 0, part), NT) + dot(wd[1, j, TQ:], piece(res, 1, part), NT)
            if d == 0:
                iown[part] = val
            else:
                isend[part, d] = val.astype(BF16)
                out.append(send(isend.at[part, d], irec.at[part, NX - d], dev(x=d)))
        return out

    def hidden_sum(part, cps):
        arrived(cps)
        total = iown[part]
        for d in range(1, NX):
            total = total + irec[part, d].astype(F32)
        hgrad[part, ix] = total.astype(BF16)
        mine = hgrad.at[part, ix]
        return [send(mine, mine, dev(x=d)) for d in (2, 1, 3)]

    def slopes(part, cps):
        arrived(cps)
        cols = pl.ds(part * CHUNK, CHUNK)
        for j in range(NX):
            grad = hgrad[part, j].astype(F32)
            units = pl.ds(j * SQ, SQ)
            pgrad[units, cols] = (grad * fac[j, part, 0].astype(F32)).astype(BF16)
            lgrad[units, cols] = (grad * fac[j, part, 1].astype(F32)).astype(BF16)

    state = gather_start(res)
    for part in P4:
        for j in range(NX):
            hm[j * SQ:(j + 1) * SQ, part * CHUNK:(part + 1) * CHUNK] = hall[part, j, TQ:HQ]
    spread(res, state, 0)
    spread(res, state, 1)
    to_core(res, state, 0)
    spread(res, state, 2)
    state[3][0].wait_recv()
    c[0] = hidden_grads(0)
    to_core(res, state, 1)
    spread(res, state, 3)
    state[3][1].wait_recv()
    c[1] = hidden_grads(1)
    to_core(res, state, 2)
    d[0] = hidden_sum(0, c[0])
    state[3][2].wait_recv()
    c[2] = hidden_grads(2)
    to_core(res, state, 3)
    d[1] = hidden_sum(1, c[1])
    state[3][3].wait_recv()
    c[3] = hidden_grads(3)
    d[2] = hidden_sum(2, c[2])
    arrived(factors)
    slopes(0, d[0])
    slopes(1, d[1])
    d[3] = hidden_sum(3, c[3])
    slopes(2, d[2])
    slopes(3, d[3])
    for cp in sent:
        cp.wait_send()


def products(tok, res, pgrad, lgrad, hm, ggate, gup, gdown, stage, sem):
    copies = []
    for n, (left, right, out) in enumerate(((hm, res, gdown), (pgrad, tok, ggate), (lgrad, tok, gup))):
        for h in range(2):
            val = dot(left[:STUD], right[h].reshape(TOKENS, HALF))
            stage[n, h] = val.astype(BF16)
            cp = pltpu.make_async_copy(stage.at[n, h], out.at[0, :, pl.ds(h * HALF, HALF)], sem.at[n, h])
            cp.start()
            copies.append(cp)
    for cp in copies:
        cp.wait()


def body(tokens, tgate, tup, tdown, sgate, sup, sdown, routes, route_weight):
    vmem, anym = pl.BlockSpec(memory_space=pltpu.VMEM), pl.BlockSpec(memory_space=pl.ANY)
    V = pltpu.VMEM
    held = (
        V((2, NZ, 64, HALF), BF16),
        V((2, NZ, 64, HALF), BF16),
        V((NX * SQ, TOKENS), BF16),
        V((NX * SQ, TOKENS), BF16),
        V((NX * SQ, TOKENS), BF16),
    )
    parts = pl.pallas_call(
        kernel,
        out_shape=held,
        in_specs=[vmem] * 3 + [anym] * 6,
        out_specs=(vmem,) * 5,
        scratch_shapes=[
            V((NX, 2 * HQ, WIDTH), BF16),
            V((2, NX, HQ, HALF), BF16),
            V((2, 8, HALF), F32),
            V((ROWS, HALF), F32),
            V((PARTS, 8, CHUNK), F32),
            V((PARTS, NX, 2 * HQ, CHUNK), BF16),
            V((PARTS, NX, 2 * HQ, CHUNK), BF16),
            V((PARTS, 2 * HQ, CHUNK), F32),
            V((PARTS, NX, HQ, CHUNK), BF16),
            V((NX, PARTS, 2, SQ, CHUNK), BF16),
            V((PARTS, CHUNK, HALF), BF16),
            V((PARTS, CHUNK, HALF), BF16),
            V((PARTS, CHUNK, HALF), F32),
            V((NZ, 64, HALF), BF16),
            V((NZ, 64, PC), BF16),
            V((PARTS, NY, SLABS, ROWS, HALF - PC), BF16),
            V((NZ, ROWS, HALF - PC), BF16),
            V((NZ, ROWS, HALF - PC), BF16),
            V((64, HALF), F32),
            V((NY, 64, PC), BF16),
            V((PARTS, NX, SQ, CHUNK), BF16),
            V((PARTS, NX, SQ, CHUNK), BF16),
            V((PARTS, SQ, CHUNK), F32),
            V((PARTS, NX, SQ, CHUNK), BF16),
            pltpu.SemaphoreType.DMA((32,)),
            pltpu.SemaphoreType.DMA((NSEM,)),
            pltpu.SemaphoreType.DMA((NSEM,)),
        ],
        compiler_params=pltpu.CompilerParams(
            collective_id=0, has_side_effects=True, vmem_limit_bytes=40 * 2**20
        ),
        cost_estimate=pl.CostEstimate(flops=6 * 10**9, bytes_accessed=12 * 10**6, transcendentals=10**6),
        name="distill",
    )(tokens, routes.T, route_weight.T, *(pltpu.with_memory_space_constraint(w, pltpu.HBM) for w in (tgate, tup, tdown, sgate, sup, sdown)))
    grad = jax.ShapeDtypeStruct((1, STUD, WIDTH), BF16)
    return pl.pallas_call(
        products,
        out_shape=(grad, grad, grad),
        in_specs=[vmem] * 5,
        out_specs=(anym,) * 3,
        scratch_shapes=[V((3, 2, STUD, HALF), BF16), pltpu.SemaphoreType.DMA((3, 2))],
        compiler_params=pltpu.CompilerParams(vmem_limit_bytes=16 * 2**20),
        cost_estimate=pl.CostEstimate(flops=15 * 10**8, bytes_accessed=3 * 10**6, transcendentals=0),
        name="products",
    )(*parts)


def solution(mesh):
    split = P(("neuron", "expert"), "dp")
    expert = P("expert", "neuron", "dp")
    return jax.shard_map(
        body,
        mesh=mesh,
        in_specs=(split, split, split, split, expert, expert, expert, P(), P()),
        out_specs=(expert, expert, expert),
        check_vma=False,
    )
```

```python
import jax
import jax.numpy as jnp
from jax import lax
from jax.experimental import pallas as pl
from jax.experimental.pallas import tpu as pltpu
from jax.sharding import PartitionSpec as P

MESH = pl.DeviceIdType.MESH
F32, BF16 = jnp.float32, jnp.bfloat16
NX, NY, NZ = 4, 4, 8
ROWS = 16
WIDTH, HALF = 2048, 1024
TEACH, STUD = 448, 224
TQ, SQ = 112, 64
HQ = TQ + SQ
CHUNK, PARTS, SLABS = 128, 4, 2
TOKENS = CHUNK * PARTS
ORDER = (0, 1, 7, 2, 6, 3, 5, 4)
POS = tuple(ORDER.index(k) for k in range(NZ))
PC = 256
ZSEND = ((7,), (1, 6), (2, 5), (3, 4))
NSEM = 176
RELAY = (1, 1, 1, 1)
NT = (((1,), (1,)), ((), ()))


PROGRAM = (
    "X0 Q1A.0 Q1A.1 P1A ",
    "Q1A.2 Q1A.3 SA.0 LW ",
    "P2A.0 P2A.1 P2A.2 LD ",
    "MIX P2A.3 SA.1 SA.2 ",
    "KA.0 SA.3 O.0 KA.1 ",
    "B.0 O.1 KA.2 B.1 ",
    "R.0 KA.3 O.2 B.2 ",
    "O.3 B.3 R.1 R.2 ",
    "R.3 A.2 A.3 A.1 ",
    "E.2 A.0 E.3 F1.2 ",
    "E.1 F1.3 E.0 F1.1 ",
    "F1.0 F2.3 F2.2 F2.1 ",
    "F2.0 FP FQ Q1G.0 ",
    "Q1G.3 Q1G.1 FF P1G ",
    "SG.0 Q1G.2 P2G.3 FAC ",
    "P2G.0 P2G.1 SG.1 SG.3 ",
    "P2G.2 KG.0 SG.2 KG.1 ",
    "H.0 KG.3 H.1 KG.2 ",
    "HM H.3 HS.0 H.2 ",
    "HS.1 HS.3 HS.2 SL.3 ",
    "SL.1 SL.0 SL.2 ",
)


def dot(a, b, dims=(((1,), (0,)), ((), ()))):
    return lax.dot_general(a, b, dims, preferred_element_type=F32)


def kernel(
    tokens, routes, weights, tgate, tup, tdown, sgate, sup, sdown,
    tok, res, pgrad, lgrad, hm,
    tin, rin, win, w1, wd, tf, blk, mix, bacc, psend, prec, pass_on, hall, fac,
    fcore, rcore, facc, fsend, rz, ry, qsend, rqz, ysend, rpy,
    isend, irec, iown, hgrad, lsem, ssem, rsem,
):
    ix, iz, ie = lax.axis_index("dp"), lax.axis_index("neuron"), lax.axis_index("expert")
    iy, ic = ie // 2, lax.rem(ie, 2)
    oc = 1 - ic

    def dev(x=0, y=0, z=0, c=0):
        core = oc if c else ic
        return (lax.rem(ix + x, NX), lax.rem(iz + z, NZ), lax.rem(iy + y, NY) * 2 + core)

    partners = (
        [dev(x=k) for k in range(1, NX)] + [dev(y=k) for k in range(1, NY)]
        + [dev(z=k) for k in range(1, NZ)] + [dev(c=1)]
    )
    barrier = pltpu.get_barrier_semaphore()
    for p in partners:
        pl.semaphore_signal(barrier, inc=1, device_id=p, device_id_type=MESH)

    loads = []

    def load(src, dst):
        cp = pltpu.make_async_copy(src, dst, lsem.at[len(loads)])
        cp.start()
        loads.append(cp)

    load(tokens, tin)
    load(routes, rin)
    load(weights, win)
    zero = jnp.zeros((SQ // 2, HALF), BF16)
    for h in range(2):
        w1[h, 3, TQ + 32:HQ] = zero
        w1[h, 3, HQ + TQ + 32:] = zero
        wd[h, 3, TQ + 32:HQ] = zero
    for j in range(NX):
        n = SQ if j < 3 else SQ // 2
        for h in range(2):
            cols = pl.ds(h * HALF, HALF)
            load(tgate.at[pl.ds(j * TQ, TQ), cols], w1.at[h, j, pl.ds(0, TQ)])
            load(sgate.at[0, pl.ds(j * SQ, n), cols], w1.at[h, j, pl.ds(TQ, n)])
            load(tup.at[pl.ds(j * TQ, TQ), cols], w1.at[h, j, pl.ds(HQ, TQ)])
            load(sup.at[0, pl.ds(j * SQ, n), cols], w1.at[h, j, pl.ds(HQ + TQ, n)])
    n_w1 = len(loads)
    for j in range(NX):
        n = SQ if j < 3 else SQ // 2
        for h in range(2):
            cols = pl.ds(h * HALF, HALF)
            load(tdown.at[pl.ds(j * TQ, TQ), cols], wd.at[h, j, pl.ds(0, TQ)])
            load(sdown.at[0, pl.ds(j * SQ, n), cols], wd.at[h, j, pl.ds(TQ, n)])
    for cp in loads[:3]:
        cp.wait()

    for h in range(2):
        tf[h] = tin[:, h * HALF:(h + 1) * HALF].astype(F32)
    blk[pl.ds(pl.multiple_of(ic * 8, 8), 8), :] = tf[ic]
    pl.semaphore_wait(barrier, len(partners))

    sent = []

    def send(src, dst, to):
        i = len(sent)
        cp = pltpu.make_async_remote_copy(
            src_ref=src, dst_ref=dst, send_sem=ssem.at[i], recv_sem=rsem.at[i],
            device_id=to, device_id_type=MESH,
        )
        cp.start()
        sent.append(cp)
        return cp

    landed = set()

    def arrived(copies):
        for c in copies:
            if id(c) not in landed:
                landed.add(id(c))
                c.wait_recv()

    def exchange():
        cp = send(tf.at[oc], blk.at[pl.ds(pl.multiple_of(ic * 8, 8), 8), :], dev(c=1))
        cp.wait_recv()
        tok[ic, 0, 0:ROWS] = blk[...].astype(BF16)

    pcols, qcols = pl.ds(0, PC), pl.ds(PC, HALF - PC)

    def rows(k):
        return pl.ds((k % NY) * ROWS, ROWS)

    def group(part):
        return pl.ds(part * SLABS, SLABS)

    cps = {}

    def gather_tasks(buf, name):
        own = buf.at[ic, 0, pl.ds(0, ROWS)]

        def y_first():
            cps["P1" + name] = [send(own.at[:, pcols], buf.at[ic, 0, rows(-k), pcols], dev(y=k)) for k in (2, 1, 3)]

        def z_first(part):
            cps["Q1" + name, part] = [
                send(own.at[:, qcols], buf.at[ic, POS[-k % NZ], pl.ds(0, ROWS), qcols], dev(z=k)) for k in ZSEND[part]
            ]

        def y_then_z(part):
            arrived(cps.pop("P1" + name, []))
            cps["P2" + name, part] = [
                send(buf.at[ic, 0, :, pcols], buf.at[ic, POS[-k % NZ], :, pcols], dev(z=k)) for k in ZSEND[part]
            ]

        def z_then_y(part):
            arrived(cps["Q1" + name, part])
            g = group(part)
            cps["S" + name, part] = [
                send(buf.at[ic, g, pl.ds(0, ROWS), qcols], buf.at[ic, g, rows(-k), qcols], dev(y=k)) for k in (2, 1, 3)
            ]

        def to_core(part):
            arrived(cps["P2" + name, part])
            arrived(cps["S" + name, part])
            cps["K" + name, part] = [send(buf.at[ic, group(part)], buf.at[ic, group(part)], dev(c=1))]

        return {"P1": y_first, "Q1": z_first, "P2": y_then_z, "S": z_then_y, "K": to_core}

    def piece(buf, h, part):
        return buf[h, part * SLABS:(part + 1) * SLABS].reshape(CHUNK, HALF)

    def own_half(part):
        arrived(cps["P2A", part])
        arrived(cps["SA", part])
        for d in range(NX):
            bacc[part, d] = dot(w1[ic, lax.rem(ix + d, NX)], piece(tok, ic, part), NT)

    def hidden_parts(part):
        arrived(cps["KA", part])
        out = []
        for d in (2, 1, 3, 0):
            val = bacc[part, d] + dot(w1[oc, lax.rem(ix + d, NX)], piece(tok, oc, part), NT)
            if d == 0 or (RELAY[part] and d != 2):
                bacc[part, d] = val
                continue
            psend[part, d] = val.astype(BF16)
            if RELAY[part]:
                cps["R", part] = [
                    send(psend.at[part, d, pl.ds(0, HQ)], pass_on.at[part, 0], dev(x=1)),
                    send(psend.at[part, d, pl.ds(HQ, HQ)], pass_on.at[part, 1], dev(x=3)),
                ]
            else:
                out.append(send(psend.at[part, d], prec.at[part, NX - d], dev(x=d)))
        cps["B", part] = out

    def relay(part):
        arrived(cps["R", part])
        for n, d in enumerate((1, 3)):
            mid = slice(n * HQ, n * HQ + HQ)
            rest = slice(HQ - n * HQ, 2 * HQ - n * HQ)
            psend[part, d, mid] = (bacc[part, d, mid] + pass_on[part, n].astype(F32)).astype(BF16)
            psend[part, d, rest] = bacc[part, d, rest].astype(BF16)
            cps["B", part].append(send(psend.at[part, d], prec.at[part, NX - d], dev(x=d)))

    def activate(part):
        arrived(cps["B", part])
        total = bacc[part, 0]
        for d in (1, 3) if RELAY[part] else (1, 2, 3):
            total = total + prec[part, d].astype(F32)
        pre, lift = total[:HQ], total[HQ:]
        s = jax.nn.sigmoid(pre)
        act = pre * s
        hidden = act * lift
        weight = mix[part, 0:1]
        hall[part, ix, 0:TQ] = (-hidden[:TQ]).astype(BF16)
        hall[part, ix, TQ:HQ] = (hidden[TQ:] * weight).astype(BF16)
        mine = hall.at[part, ix]
        cps["A", part] = [send(mine, mine, dev(x=d)) for d in (2, 1, 3)]
        slope = s * (1.0 + pre * (1.0 - s))
        fac[ix, part, 0] = (weight * (lift * slope)[TQ:]).astype(BF16)
        fac[ix, part, 1] = (weight * act[TQ:]).astype(BF16)

    def factors():
        cps["FAC"] = [send(fac.at[ix], fac.at[ix], dev(x=k)) for k in (2, 1, 3)]

    def outputs(part):
        arrived(cps["A", part])
        hidden = hall[part].reshape(NX * HQ, CHUNK).T
        fcore[part] = dot(hidden, wd[oc].reshape(NX * HQ, HALF)).astype(BF16)
        cps["E", part] = [send(fcore.at[part], rcore.at[part], dev(c=1))]
        facc[part] = dot(hidden, wd[ic].reshape(NX * HQ, HALF))

    def scatter_first(part):
        arrived(cps["E", part])
        total = facc[part] + rcore[part].astype(F32)
        facc[part] = total
        fsend[part * SLABS:(part + 1) * SLABS] = total.astype(BF16).reshape(SLABS, 64, HALF)
        cps["F1", part] = [
            send(fsend.at[group(part), rows(k), qcols], ry.at[part, NY - k], dev(y=k)) for k in (2, 1, 3)
        ]
        cps["F1P", part] = [
            send(fsend.at[pos, :, pcols], rz.at[POS[-ORDER[pos] % NZ]], dev(z=ORDER[pos]))
            for pos in range(part * SLABS, (part + 1) * SLABS) if ORDER[pos]
        ]

    def scatter_second(part):
        arrived(cps["F1", part])
        total = facc[part].reshape(SLABS, 64, HALF)[:, :ROWS, PC:]
        for d in range(1, NY):
            total = total + ry[part, d].astype(F32)
        if part == 0:
            ysend[0:ROWS, PC:] = total[0]
        qsend[part * SLABS:(part + 1) * SLABS] = total.astype(BF16)
        cps["F2", part] = [
            send(qsend.at[pos], rqz.at[POS[-ORDER[pos] % NZ]], dev(z=ORDER[pos]))
            for pos in range(part * SLABS, (part + 1) * SLABS) if ORDER[pos]
        ]

    def scatter_y():
        total = facc[0, 0:64, :PC]
        for part in range(PARTS):
            arrived(cps["F1P", part])
        for pos in range(1, NZ):
            total = total + rz[pos].astype(F32)
        ysend[:, :PC] = total
        rpy[0] = total.astype(BF16)
        cps["FP"] = [send(rpy.at[0, rows(k)], rpy.at[NY - k, pl.ds(0, ROWS)], dev(y=k)) for k in (2, 1, 3)]

    def residual_q():
        for part in range(PARTS):
            arrived(cps["F2", part])
        total = ysend[0:ROWS, PC:]
        for pos in range(1, NZ):
            total = total + rqz[pos].astype(F32)
        res[ic, 0, 0:ROWS, PC:] = total.astype(BF16)

    def residual_p():
        arrived(cps["FP"])
        total = ysend[0:ROWS, :PC]
        for k in range(1, NY):
            total = total + rpy[k, 0:ROWS].astype(F32)
        res[ic, 0, 0:ROWS, :PC] = total.astype(BF16)

    def mixing():
        m = jnp.sum(jnp.where(rin[...] == ie, win[...], 0.0), axis=0, keepdims=True)
        m = jnp.broadcast_to(m, (8, TOKENS))
        m = pltpu.roll(m, lax.rem(NZ - iz, NZ) * 64, 1)
        lane = lax.broadcasted_iota(jnp.int32, (8, TOKENS), 1)
        near = pltpu.roll(m, lax.rem(TOKENS - iy * ROWS, TOKENS), 1)
        far = pltpu.roll(m, 64 - iy * ROWS, 1)
        m = jnp.where(lax.rem(lane, 64) < 64 - iy * ROWS, near, far)
        low = lax.broadcasted_iota(jnp.int32, (8, CHUNK), 1) < 64
        for part in range(PARTS):
            two = []
            for side in range(2):
                k = ORDER[part * 2 + side]
                t = m[:, (k // 2) * CHUNK:(k // 2 + 1) * CHUNK]
                two.append(t if k % 2 == side else pltpu.roll(t, 64, 1))
            mix[part] = jnp.where(low, two[0], two[1])

    def hidden_grads(part):
        arrived(cps["KG", part])
        out = []
        for d in (2, 1, 3, 0):
            j = lax.rem(ix + d, NX)
            val = dot(wd[0, j, TQ:], piece(res, 0, part), NT) + dot(wd[1, j, TQ:], piece(res, 1, part), NT)
            if d == 0:
                iown[part] = val
            else:
                isend[part, d] = val.astype(BF16)
                out.append(send(isend.at[part, d], irec.at[part, NX - d], dev(x=d)))
        cps["H", part] = out

    def hidden_sum(part):
        arrived(cps["H", part])
        total = iown[part]
        for d in range(1, NX):
            total = total + irec[part, d].astype(F32)
        hgrad[part, ix] = total.astype(BF16)
        mine = hgrad.at[part, ix]
        cps["HS", part] = [send(mine, mine, dev(x=d)) for d in (2, 1, 3)]

    def slopes(part):
        arrived(cps["HS", part])
        arrived(cps.pop("FAC", []))
        cols = pl.ds(part * CHUNK, CHUNK)
        for j in range(NX):
            grad = hgrad[part, j].astype(F32)
            units = pl.ds(j * SQ, SQ)
            pgrad[units, cols] = (grad * fac[j, part, 0].astype(F32)).astype(BF16)
            lgrad[units, cols] = (grad * fac[j, part, 1].astype(F32)).astype(BF16)

    def weighted_hidden():
        for part in range(PARTS):
            for j in range(NX):
                hm[j * SQ:(j + 1) * SQ, part * CHUNK:(part + 1) * CHUNK] = hall[part, j, TQ:HQ]

    def weights_ready(first, last):
        for cp in loads[first:last]:
            cp.wait()

    tasks = {
        "X0": exchange, "MIX": mixing, "HM": weighted_hidden, "FAC": factors,
        "LW": lambda: weights_ready(3, n_w1), "LD": lambda: weights_ready(n_w1, None),
        "O": own_half, "B": hidden_parts, "R": relay, "A": activate, "E": outputs, "F1": scatter_first,
        "F2": scatter_second, "FP": scatter_y, "FQ": residual_q, "FF": residual_p, "H": hidden_grads,
        "HS": hidden_sum, "SL": slopes,
    }
    for name, buf in (("A", tok), ("G", res)):
        tasks.update({key + name: task for key, task in gather_tasks(buf, name).items()})
    for step in ("".join(PROGRAM)).split():
        key, _, part = step.partition(".")
        tasks[key](*([int(part)] if part else []))
    for cp in sent:
        cp.wait_send()


def products(tok, res, pgrad, lgrad, hm, ggate, gup, gdown, stage, sem):
    copies = []
    for n, (left, right, out) in enumerate(((hm, res, gdown), (pgrad, tok, ggate), (lgrad, tok, gup))):
        for h in range(2):
            val = dot(left[:STUD], right[h].reshape(TOKENS, HALF))
            stage[n, h] = val.astype(BF16)
            cp = pltpu.make_async_copy(stage.at[n, h], out.at[0, :, pl.ds(h * HALF, HALF)], sem.at[n, h])
            cp.start()
            copies.append(cp)
    for cp in copies:
        cp.wait()


def body(tokens, tgate, tup, tdown, sgate, sup, sdown, routes, route_weight):
    vmem, anym = pl.BlockSpec(memory_space=pltpu.VMEM), pl.BlockSpec(memory_space=pl.ANY)
    V = pltpu.VMEM
    held = (
        V((2, NZ, 64, HALF), BF16),
        V((2, NZ, 64, HALF), BF16),
        V((NX * SQ, TOKENS), BF16),
        V((NX * SQ, TOKENS), BF16),
        V((NX * SQ, TOKENS), BF16),
    )
    args = (tokens, routes.T, route_weight.T, tgate, tup, tdown, sgate, sup, sdown)
    parts = pl.pallas_call(
        kernel,
        out_shape=held,
        in_specs=[anym] * 9,
        out_specs=(vmem,) * 5,
        scratch_shapes=[
            V((8, WIDTH), BF16),
            V((2, TOKENS), jnp.int32),
            V((2, TOKENS), F32),
            V((2, NX, 2 * HQ, HALF), BF16),
            V((2, NX, HQ, HALF), BF16),
            V((2, 8, HALF), F32),
            V((ROWS, HALF), F32),
            V((PARTS, 8, CHUNK), F32),
            V((PARTS, NX, 2 * HQ, CHUNK), F32),
            V((PARTS, NX, 2 * HQ, CHUNK), BF16),
            V((PARTS, NX, 2 * HQ, CHUNK), BF16),
            V((PARTS, 2, HQ, CHUNK), BF16),
            V((PARTS, NX, HQ, CHUNK), BF16),
            V((NX, PARTS, 2, SQ, CHUNK), BF16),
            V((PARTS, CHUNK, HALF), BF16),
            V((PARTS, CHUNK, HALF), BF16),
            V((PARTS, CHUNK, HALF), F32),
            V((NZ, 64, HALF), BF16),
            V((NZ, 64, PC), BF16),
            V((PARTS, NY, SLABS, ROWS, HALF - PC), BF16),
            V((NZ, ROWS, HALF - PC), BF16),
            V((NZ, ROWS, HALF - PC), BF16),
            V((64, HALF), F32),
            V((NY, 64, PC), BF16),
            V((PARTS, NX, SQ, CHUNK), BF16),
            V((PARTS, NX, SQ, CHUNK), BF16),
            V((PARTS, SQ, CHUNK), F32),
            V((PARTS, NX, SQ, CHUNK), BF16),
            pltpu.SemaphoreType.DMA((64,)),
            pltpu.SemaphoreType.DMA((NSEM,)),
            pltpu.SemaphoreType.DMA((NSEM,)),
        ],
        compiler_params=pltpu.CompilerParams(
            collective_id=0, has_side_effects=True, vmem_limit_bytes=40 * 2**20
        ),
        cost_estimate=pl.CostEstimate(flops=6 * 10**9, bytes_accessed=12 * 10**6, transcendentals=10**6),
        name="distill",
    )(*(pltpu.with_memory_space_constraint(a, pltpu.HBM) for a in args))
    grad = jax.ShapeDtypeStruct((1, STUD, WIDTH), BF16)
    return pl.pallas_call(
        products,
        out_shape=(grad, grad, grad),
        in_specs=[vmem] * 5,
        out_specs=(anym,) * 3,
        scratch_shapes=[V((3, 2, STUD, HALF), BF16), pltpu.SemaphoreType.DMA((3, 2))],
        compiler_params=pltpu.CompilerParams(vmem_limit_bytes=16 * 2**20),
        cost_estimate=pl.CostEstimate(flops=15 * 10**8, bytes_accessed=3 * 10**6, transcendentals=0),
        name="products",
    )(*parts)


def solution(mesh):
    split = P(("neuron", "expert"), "dp")
    expert = P("expert", "neuron", "dp")
    return jax.shard_map(
        body,
        mesh=mesh,
        in_specs=(split, split, split, split, expert, expert, expert, P(), P()),
        out_specs=(expert, expert, expert),
        check_vma=False,
    )
```

```python
import jax
import jax.numpy as jnp
from jax import lax
from jax.experimental import pallas as pl
from jax.experimental.pallas import tpu as pltpu
from jax.sharding import PartitionSpec as P

MESH = pl.DeviceIdType.MESH
F32, BF16 = jnp.float32, jnp.bfloat16
NX, NY, NZ = 4, 4, 8
ROWS = 16
WIDTH, HALF = 2048, 1024
TEACH, STUD = 448, 224
TQ, SQ = 112, 64
HQ = TQ + SQ
CHUNK, PARTS, SLABS = 128, 4, 2
TOKENS = CHUNK * PARTS
ORDER = (0, 1, 7, 2, 6, 3, 5, 4)
POS = tuple(ORDER.index(k) for k in range(NZ))
PC = 256
ZSEND = ((7,), (1, 6), (2, 5), (3, 4))
NSEM = 176
DRELAY = (0, 0, 0, 0)
DIRECT = (0, 0, 0, 1)
RELAY = (1, 1, 1, 1)
NT = (((1,), (1,)), ((), ()))


PROGRAM = (
    "X0 Q1A.0 Q1A.1 Q1A.3 ",
    "P1A LD1 Q1A.2 SA.0 ",
    "P2A.0 P2A.1 P2A.3 P2A.2 ",
    "LD2 SA.1 SA.3 KA.0 ",
    "O.0 SA.2 KA.1 B.0 ",
    "O.1 KA.3 B.1 R.0 ",
    "KA.2 O.3 MIX B.3 ",
    "O.2 B.2 A.0 R.3 ",
    "R.2 R.1 A.3 E.0 ",
    "A.2 A.1 F1.0 E.3 ",
    "E.2 F1.3 E.1 F1.2 ",
    "F2.0 F1.1 HM F2.3 ",
    "F2.2 F2.1 FAC FP ",
    "FQ Q1G.0 FF Q1G.1 ",
    "P1G Q1G.2 Q1G.3 SG.0 ",
    "P2G.0 P2G.1 P2G.3 SG.1 ",
    "P2G.2 SG.2 KG.0 SG.3 ",
    "KG.1 H.0 KG.2 H.1 ",
    "KG.3 HS.0 H.2 H.3 ",
    "HS.1 HS.2 GD SL.1 ",
    "SL.3 SL.0 SL.2 ",
)


def dot(a, b, dims=(((1,), (0,)), ((), ()))):
    return lax.dot_general(a, b, dims, preferred_element_type=F32)


def kernel(
    tokens, routes, weights, tgate, tup, tdown, sgate, sup, sdown,
    tok, gd, pgrad, lgrad,
    res, hm, tin, rin, win, w1, wd, tf, blk, mix, bacc, psend, prec, pass_on, hall, fac,
    fcore, rcore, facc, fsend, rz, ry, qsend, rqz, ysend, rpy,
    isend, irec, iall, iown, hgrad, lsem, ssem, rsem,
):
    ix, iz, ie = lax.axis_index("dp"), lax.axis_index("neuron"), lax.axis_index("expert")
    iy, ic = ie // 2, lax.rem(ie, 2)
    oc = 1 - ic

    def dev(x=0, y=0, z=0, c=0):
        core = oc if c else ic
        return (lax.rem(ix + x, NX), lax.rem(iz + z, NZ), lax.rem(iy + y, NY) * 2 + core)

    partners = (
        [dev(x=k) for k in range(1, NX)] + [dev(y=k) for k in range(1, NY)]
        + [dev(z=k) for k in range(1, NZ)] + [dev(c=1)]
    )
    barrier = pltpu.get_barrier_semaphore()
    for p in partners:
        pl.semaphore_signal(barrier, inc=1, device_id=p, device_id_type=MESH)

    loads = []

    def load(src, dst):
        cp = pltpu.make_async_copy(src, dst, lsem.at[len(loads)])
        cp.start()
        loads.append(cp)

    load(tokens, tin)
    load(routes, rin)
    load(weights, win)
    n_w1, n_all = 3 + 8 * NX, 3 + 12 * NX

    def load_first():
        zero = jnp.zeros((SQ // 2, HALF), BF16)
        for h in range(2):
            w1[h, 3, TQ + 32:HQ] = zero
            w1[h, 3, HQ + TQ + 32:] = zero
        for j in range(NX):
            n = SQ if j < 3 else SQ // 2
            for h in range(2):
                cols = pl.ds(h * HALF, HALF)
                load(tgate.at[pl.ds(j * TQ, TQ), cols], w1.at[h, j, pl.ds(0, TQ)])
                load(sgate.at[0, pl.ds(j * SQ, n), cols], w1.at[h, j, pl.ds(TQ, n)])
                load(tup.at[pl.ds(j * TQ, TQ), cols], w1.at[h, j, pl.ds(HQ, TQ)])
                load(sup.at[0, pl.ds(j * SQ, n), cols], w1.at[h, j, pl.ds(HQ + TQ, n)])

    def load_down():
        zero = jnp.zeros((SQ // 2, HALF), BF16)
        for h in range(2):
            wd[h, 3, TQ + 32:HQ] = zero
        for j in range(NX):
            n = SQ if j < 3 else SQ // 2
            for h in range(2):
                cols = pl.ds(h * HALF, HALF)
                load(tdown.at[pl.ds(j * TQ, TQ), cols], wd.at[h, j, pl.ds(0, TQ)])
                load(sdown.at[0, pl.ds(j * SQ, n), cols], wd.at[h, j, pl.ds(TQ, n)])

    loaded = set()

    def weights_ready(first, last):
        for i in range(first, last):
            if i not in loaded:
                loaded.add(i)
                loads[i].wait()

    weights_ready(0, 3)

    for h in range(2):
        tf[h] = tin[:, h * HALF:(h + 1) * HALF].astype(F32)
    blk[pl.ds(pl.multiple_of(ic * 8, 8), 8), :] = tf[ic]
    pl.semaphore_wait(barrier, len(partners))

    sent = []

    def send(src, dst, to):
        i = len(sent)
        cp = pltpu.make_async_remote_copy(
            src_ref=src, dst_ref=dst, send_sem=ssem.at[i], recv_sem=rsem.at[i],
            device_id=to, device_id_type=MESH,
        )
        cp.start()
        sent.append(cp)
        return cp

    landed = set()

    def arrived(copies):
        for c in copies:
            if id(c) not in landed:
                landed.add(id(c))
                c.wait_recv()

    def exchange():
        cp = send(tf.at[oc], blk.at[pl.ds(pl.multiple_of(ic * 8, 8), 8), :], dev(c=1))
        cp.wait_recv()
        tok[ic, 0, 0:ROWS] = blk[...].astype(BF16)

    pcols, qcols = pl.ds(0, PC), pl.ds(PC, HALF - PC)

    def rows(k):
        return pl.ds((k % NY) * ROWS, ROWS)

    def group(part):
        return pl.ds(part * SLABS, SLABS)

    cps = {}

    def gather_tasks(buf, name):
        own = buf.at[ic, 0, pl.ds(0, ROWS)]

        def y_first():
            cps["P1" + name] = [send(own.at[:, pcols], buf.at[ic, 0, rows(-k), pcols], dev(y=k)) for k in (2, 1, 3)]

        def z_first(part):
            cps["Q1" + name, part] = [
                send(own.at[:, qcols], buf.at[ic, POS[-k % NZ], pl.ds(0, ROWS), qcols], dev(z=k)) for k in ZSEND[part]
            ]

        def y_then_z(part):
            arrived(cps.pop("P1" + name, []))
            cps["P2" + name, part] = [
                send(buf.at[ic, 0, :, pcols], buf.at[ic, POS[-k % NZ], :, pcols], dev(z=k)) for k in ZSEND[part]
            ]

        def z_then_y(part):
            arrived(cps["Q1" + name, part])
            g = group(part)
            cps["S" + name, part] = [
                send(buf.at[ic, g, pl.ds(0, ROWS), qcols], buf.at[ic, g, rows(-k), qcols], dev(y=k)) for k in (2, 1, 3)
            ]

        def to_core(part):
            arrived(cps["P2" + name, part])
            arrived(cps["S" + name, part])
            cps["K" + name, part] = [send(buf.at[ic, group(part)], buf.at[ic, group(part)], dev(c=1))]

        return {"P1": y_first, "Q1": z_first, "P2": y_then_z, "S": z_then_y, "K": to_core}

    def piece(buf, h, part):
        return buf[h, part * SLABS:(part + 1) * SLABS].reshape(CHUNK, HALF)

    def own_half(part):
        weights_ready(3, n_w1)
        arrived(cps["P2A", part])
        arrived(cps["SA", part])
        for d in range(NX):
            bacc[part, d] = dot(w1[ic, lax.rem(ix + d, NX)], piece(tok, ic, part), NT)

    def hidden_parts(part):
        arrived(cps["KA", part])
        out = []
        for d in (2, 1, 3, 0):
            val = bacc[part, d] + dot(w1[oc, lax.rem(ix + d, NX)], piece(tok, oc, part), NT)
            if d == 0 or (RELAY[part] and d != 2):
                bacc[part, d] = val
                continue
            psend[part, d] = val.astype(BF16)
            if RELAY[part]:
                cps["R", part] = [
                    send(psend.at[part, d, pl.ds(0, HQ)], pass_on.at[part, 0], dev(x=1)),
                    send(psend.at[part, d, pl.ds(HQ, HQ)], pass_on.at[part, 1], dev(x=3)),
                ]
            else:
                out.append(send(psend.at[part, d], prec.at[part, NX - d], dev(x=d)))
        cps["B", part] = out

    def relay(part):
        arrived(cps["R", part])
        for n, d in enumerate((1, 3)):
            mid = slice(n * HQ, n * HQ + HQ)
            rest = slice(HQ - n * HQ, 2 * HQ - n * HQ)
            psend[part, d, mid] = (bacc[part, d, mid] + pass_on[part, n].astype(F32)).astype(BF16)
            psend[part, d, rest] = bacc[part, d, rest].astype(BF16)
            cps["B", part].append(send(psend.at[part, d], prec.at[part, NX - d], dev(x=d)))

    def activate(part):
        arrived(cps["B", part])
        total = bacc[part, 0]
        for d in (1, 3) if RELAY[part] else (1, 2, 3):
            total = total + prec[part, d].astype(F32)
        pre, lift = total[:HQ], total[HQ:]
        s = jax.nn.sigmoid(pre)
        act = pre * s
        hidden = act * lift
        weight = mix[part, 0:1]
        hall[part, ix, 0:TQ] = (-hidden[:TQ]).astype(BF16)
        hall[part, ix, TQ:HQ] = (hidden[TQ:] * weight).astype(BF16)
        mine = hall.at[part, ix]
        cps["A", part] = [send(mine, mine, dev(x=d)) for d in ((1, 3) if DRELAY[part] else (2, 1, 3))]
        slope = s * (1.0 + pre * (1.0 - s))
        fac[ix, part, 0] = (weight * (lift * slope)[TQ:]).astype(BF16)
        fac[ix, part, 1] = (weight * act[TQ:]).astype(BF16)

    def factors():
        cps["FAC"] = [send(fac.at[ix], fac.at[ix], dev(x=k)) for k in (2, 1, 3)]

    def pass_hidden(part):
        arrived(cps["A", part])
        cps["DR", part] = []
        for d, first, n in ((1, 0, 96), (3, 96, HQ - 96)):
            piece_of = hall.at[part, lax.rem(ix + NX - d, NX), pl.ds(first, n)]
            cps["DR", part].append(send(piece_of, piece_of, dev(x=d)))

    def outputs(part):
        weights_ready(n_w1, n_all)
        arrived(cps["A", part])
        arrived(cps.get(("DR", part), []))
        hidden = hall[part].reshape(NX * HQ, CHUNK).T
        fcore[part] = dot(hidden, wd[oc].reshape(NX * HQ, HALF)).astype(BF16)
        cps["E", part] = [send(fcore.at[part], rcore.at[part], dev(c=1))]
        facc[part] = dot(hidden, wd[ic].reshape(NX * HQ, HALF))

    def scatter_first(part):
        arrived(cps["E", part])
        total = facc[part] + rcore[part].astype(F32)
        facc[part] = total
        fsend[part * SLABS:(part + 1) * SLABS] = total.astype(BF16).reshape(SLABS, 64, HALF)
        cps["F1", part] = [
            send(fsend.at[group(part), rows(k), qcols], ry.at[part, NY - k], dev(y=k)) for k in (2, 1, 3)
        ]
        cps["F1P", part] = [
            send(fsend.at[pos, :, pcols], rz.at[POS[-ORDER[pos] % NZ]], dev(z=ORDER[pos]))
            for pos in range(part * SLABS, (part + 1) * SLABS) if ORDER[pos]
        ]

    def scatter_second(part):
        arrived(cps["F1", part])
        total = facc[part].reshape(SLABS, 64, HALF)[:, :ROWS, PC:]
        for d in range(1, NY):
            total = total + ry[part, d].astype(F32)
        if part == 0:
            ysend[0:ROWS, PC:] = total[0]
        qsend[part * SLABS:(part + 1) * SLABS] = total.astype(BF16)
        cps["F2", part] = [
            send(qsend.at[pos], rqz.at[POS[-ORDER[pos] % NZ]], dev(z=ORDER[pos]))
            for pos in range(part * SLABS, (part + 1) * SLABS) if ORDER[pos]
        ]

    def scatter_y():
        total = facc[0, 0:64, :PC]
        for part in range(PARTS):
            arrived(cps["F1P", part])
        for pos in range(1, NZ):
            total = total + rz[pos].astype(F32)
        ysend[:, :PC] = total
        rpy[0] = total.astype(BF16)
        cps["FP"] = [send(rpy.at[0, rows(k)], rpy.at[NY - k, pl.ds(0, ROWS)], dev(y=k)) for k in (2, 1, 3)]

    def residual_q():
        for part in range(PARTS):
            arrived(cps["F2", part])
        total = ysend[0:ROWS, PC:]
        for pos in range(1, NZ):
            total = total + rqz[pos].astype(F32)
        res[ic, 0, 0:ROWS, PC:] = total.astype(BF16)

    def residual_p():
        arrived(cps["FP"])
        total = ysend[0:ROWS, :PC]
        for k in range(1, NY):
            total = total + rpy[k, 0:ROWS].astype(F32)
        res[ic, 0, 0:ROWS, :PC] = total.astype(BF16)

    def mixing():
        m = jnp.sum(jnp.where(rin[...] == ie, win[...], 0.0), axis=0, keepdims=True)
        m = jnp.broadcast_to(m, (8, TOKENS))
        m = pltpu.roll(m, lax.rem(NZ - iz, NZ) * 64, 1)
        lane = lax.broadcasted_iota(jnp.int32, (8, TOKENS), 1)
        near = pltpu.roll(m, lax.rem(TOKENS - iy * ROWS, TOKENS), 1)
        far = pltpu.roll(m, 64 - iy * ROWS, 1)
        m = jnp.where(lax.rem(lane, 64) < 64 - iy * ROWS, near, far)
        low = lax.broadcasted_iota(jnp.int32, (8, CHUNK), 1) < 64
        for part in range(PARTS):
            two = []
            for side in range(2):
                k = ORDER[part * 2 + side]
                t = m[:, (k // 2) * CHUNK:(k // 2 + 1) * CHUNK]
                two.append(t if k % 2 == side else pltpu.roll(t, 64, 1))
            mix[part] = jnp.where(low, two[0], two[1])

    def hidden_grads(part):
        arrived(cps["KG", part])
        left = [wd[h, :, TQ:].reshape(NX * SQ, HALF) for h in range(2)]
        val = dot(left[0], piece(res, 0, part), NT) + dot(left[1], piece(res, 1, part), NT)
        iown[part] = val.reshape(NX, SQ, CHUNK)
        isend[part] = val.astype(BF16).reshape(NX, SQ, CHUNK)
        if DIRECT[part]:
            out = [send(isend.at[part], iall.at[part, NX - d], dev(x=d)) for d in (2, 1, 3)]
        else:
            out = [
                send(isend.at[part, lax.rem(ix + d, NX)], irec.at[part, NX - d], dev(x=d)) for d in (2, 1, 3)
            ]
        cps["H", part] = out

    def hidden_sum(part):
        arrived(cps["H", part])
        total = iown[part, ix]
        for d in range(1, NX):
            total = total + irec[part, d].astype(F32)
        hgrad[part, ix] = total.astype(BF16)
        mine = hgrad.at[part, ix]
        cps["HS", part] = [send(mine, mine, dev(x=d)) for d in (2, 1, 3)]

    def slopes(part):
        arrived(cps["H" if DIRECT[part] else "HS", part])
        arrived(cps["FAC"])
        cols = pl.ds(part * CHUNK, CHUNK)
        if DIRECT[part]:
            grad = iown[part].reshape(NX * SQ, CHUNK)
            for d in range(1, NX):
                grad = grad + iall[part, d].reshape(NX * SQ, CHUNK).astype(F32)
            pgrad[:, cols] = (grad * fac[:, part, 0].reshape(NX * SQ, CHUNK).astype(F32)).astype(BF16)
            lgrad[:, cols] = (grad * fac[:, part, 1].reshape(NX * SQ, CHUNK).astype(F32)).astype(BF16)
            return
        for j in range(NX):
            grad = hgrad[part, j].astype(F32)
            units = pl.ds(j * SQ, SQ)
            pgrad[units, cols] = (grad * fac[j, part, 0].astype(F32)).astype(BF16)
            lgrad[units, cols] = (grad * fac[j, part, 1].astype(F32)).astype(BF16)

    def weighted_hidden():
        for part in range(PARTS):
            for j in range(NX):
                hm[j * SQ:(j + 1) * SQ, part * CHUNK:(part + 1) * CHUNK] = hall[part, j, TQ:HQ]

    def down_product():
        for h in range(2):
            gd[h] = dot(hm[:STUD], res[h].reshape(TOKENS, HALF)).astype(BF16)

    tasks = {
        "X0": exchange, "MIX": mixing, "HM": weighted_hidden, "FAC": factors,
        "LD1": load_first, "LD2": load_down, "DR": pass_hidden, "GD": down_product,
        "O": own_half, "B": hidden_parts, "R": relay, "A": activate, "E": outputs, "F1": scatter_first,
        "F2": scatter_second, "FP": scatter_y, "FQ": residual_q, "FF": residual_p, "H": hidden_grads,
        "HS": hidden_sum, "SL": slopes,
    }
    for name, buf in (("A", tok), ("G", res)):
        tasks.update({key + name: task for key, task in gather_tasks(buf, name).items()})
    for step in ("".join(PROGRAM)).split():
        key, _, part = step.partition(".")
        tasks[key](*([int(part)] if part else []))
    for cp in sent:
        cp.wait_send()


def products(tok, gd, pgrad, lgrad, ggate, gup, gdown, stage, sem):
    copies = []

    def write(src, out, n, h):
        cp = pltpu.make_async_copy(src, out.at[0, :, pl.ds(h * HALF, HALF)], sem.at[n, h])
        cp.start()
        copies.append(cp)

    for h in range(2):
        write(gd.at[h], gdown, 2, h)
    for n, (left, out) in enumerate(((pgrad, ggate), (lgrad, gup))):
        for h in range(2):
            stage[n, h] = dot(left[:STUD], tok[h].reshape(TOKENS, HALF)).astype(BF16)
            write(stage.at[n, h], out, n, h)
    for cp in copies:
        cp.wait()


def body(tokens, tgate, tup, tdown, sgate, sup, sdown, routes, route_weight):
    vmem, anym = pl.BlockSpec(memory_space=pltpu.VMEM), pl.BlockSpec(memory_space=pl.ANY)
    V = pltpu.VMEM
    held = (
        V((2, NZ, 64, HALF), BF16),
        V((2, STUD, HALF), BF16),
        V((NX * SQ, TOKENS), BF16),
        V((NX * SQ, TOKENS), BF16),
    )
    args = (tokens, routes.T, route_weight.T, tgate, tup, tdown, sgate, sup, sdown)
    parts = pl.pallas_call(
        kernel,
        out_shape=held,
        in_specs=[anym] * 9,
        out_specs=(vmem,) * 4,
        scratch_shapes=[
            V((2, NZ, 64, HALF), BF16),
            V((NX * SQ, TOKENS), BF16),
            V((8, WIDTH), BF16),
            V((2, TOKENS), jnp.int32),
            V((2, TOKENS), F32),
            V((2, NX, 2 * HQ, HALF), BF16),
            V((2, NX, HQ, HALF), BF16),
            V((2, 8, HALF), F32),
            V((ROWS, HALF), F32),
            V((PARTS, 8, CHUNK), F32),
            V((PARTS, NX, 2 * HQ, CHUNK), F32),
            V((PARTS, NX, 2 * HQ, CHUNK), BF16),
            V((PARTS, NX, 2 * HQ, CHUNK), BF16),
            V((PARTS, 2, HQ, CHUNK), BF16),
            V((PARTS, NX, HQ, CHUNK), BF16),
            V((NX, PARTS, 2, SQ, CHUNK), BF16),
            V((PARTS, CHUNK, HALF), BF16),
            V((PARTS, CHUNK, HALF), BF16),
            V((PARTS, CHUNK, HALF), F32),
            V((NZ, 64, HALF), BF16),
            V((NZ, 64, PC), BF16),
            V((PARTS, NY, SLABS, ROWS, HALF - PC), BF16),
            V((NZ, ROWS, HALF - PC), BF16),
            V((NZ, ROWS, HALF - PC), BF16),
            V((64, HALF), F32),
            V((NY, 64, PC), BF16),
            V((PARTS, NX, SQ, CHUNK), BF16),
            V((PARTS, NX, SQ, CHUNK), BF16),
            V((PARTS, NX, NX, SQ, CHUNK), BF16),
            V((PARTS, NX, SQ, CHUNK), F32),
            V((PARTS, NX, SQ, CHUNK), BF16),
            pltpu.SemaphoreType.DMA((64,)),
            pltpu.SemaphoreType.DMA((NSEM,)),
            pltpu.SemaphoreType.DMA((NSEM,)),
        ],
        compiler_params=pltpu.CompilerParams(
            collective_id=0, has_side_effects=True, vmem_limit_bytes=40 * 2**20
        ),
        cost_estimate=pl.CostEstimate(flops=6 * 10**9, bytes_accessed=12 * 10**6, transcendentals=10**6),
        name="distill",
    )(*(pltpu.with_memory_space_constraint(a, pltpu.HBM) for a in args))
    grad = jax.ShapeDtypeStruct((1, STUD, WIDTH), BF16)
    return pl.pallas_call(
        products,
        out_shape=(grad, grad, grad),
        in_specs=[vmem] * 4,
        out_specs=(anym,) * 3,
        scratch_shapes=[V((2, 2, STUD, HALF), BF16), pltpu.SemaphoreType.DMA((3, 2))],
        compiler_params=pltpu.CompilerParams(vmem_limit_bytes=16 * 2**20),
        cost_estimate=pl.CostEstimate(flops=15 * 10**8, bytes_accessed=3 * 10**6, transcendentals=0),
        name="products",
    )(*parts)


def solution(mesh):
    split = P(("neuron", "expert"), "dp")
    expert = P("expert", "neuron", "dp")
    return jax.shard_map(
        body,
        mesh=mesh,
        in_specs=(split, split, split, split, expert, expert, expert, P(), P()),
        out_specs=(expert, expert, expert),
        check_vma=False,
    )
```

```python
import jax
import jax.numpy as jnp
from jax import lax
from jax.experimental import pallas as pl
from jax.experimental.pallas import tpu as pltpu
from jax.sharding import PartitionSpec as P

MESH = pl.DeviceIdType.MESH
F32, BF16 = jnp.float32, jnp.bfloat16
NX, NY, NZ = 4, 4, 8
ROWS = 16
WIDTH, HALF = 2048, 1024
TEACH, STUD = 448, 224
TQ, SQ = 112, 64
HQ = TQ + SQ
CHUNK, PARTS, SLABS = 128, 4, 2
TOKENS = CHUNK * PARTS
ORDER = (0, 1, 7, 2, 6, 3, 5, 4)
POS = tuple(ORDER.index(k) for k in range(NZ))
PC = 256
ZSEND = ((7,), (1, 6), (2, 5), (3, 4))
NSEM = 192
DRELAY = (0, 0, 0, 0)
DIRECT = (0, 1, 1, 0)
RELAY = (1, 1, 1, 1)
NT = (((1,), (1,)), ((), ()))


PROGRAM = (
    "X0 Q1A.0 Q1A.2 Q1A.3 ",
    "P1A LD1 MIX Q1A.1 ",
    "SA.0 P2A.0 P2A.2 P2A.3 ",
    "LD2 SA.2 KA.0 SA.3 ",
    "P2A.1 O.0 SA.1 B.0 ",
    "KA.2 O.2 B.2 KA.3 ",
    "R.0 O.3 KA.1 O.1 ",
    "B.3 B.1 R.2 R.3 ",
    "R.1 A.2 A.3 A.1 ",
    "A.0 E.2 E.3 F1.2 ",
    "E.1 F1.3 E.0 FAC ",
    "F1.1 F1.0 F2.3 F2.2 ",
    "F2.1 F2.0 FP FQ ",
    "Q1G.0 Q1G.1 FF Q1G.3 ",
    "P1G Q1G.2 SG.0 P2G.1 ",
    "P2G.0 P2G.3 SG.1 P2G.2 ",
    "SG.3 KG.0 SG.2 KG.1 ",
    "H.0 HM H.1 KG.3 ",
    "KG.2 H.3 HS.0 H.2 ",
    "HS.3 SL.0 GD SL.2 ",
    "SL.1 SL.3 ",
)


def dot(a, b, dims=(((1,), (0,)), ((), ()))):
    return lax.dot_general(a, b, dims, preferred_element_type=F32)


def kernel(
    tokens, routes, weights, tgate, tup, tdown, sgate, sup, sdown,
    tok, gd, pgrad, lgrad,
    res, hm, tin, rin, win, w1, wd, tf, blk, mix, bacc, psend, prec, pass_on, hall, fac,
    fcore, rcore, facc, fsend, rz, ry, qsend, rqz, ysend, rpy,
    isend, irec, iall, iown, hgrad, lsem, ssem, rsem,
):
    ix, iz, ie = lax.axis_index("dp"), lax.axis_index("neuron"), lax.axis_index("expert")
    iy, ic = ie // 2, lax.rem(ie, 2)
    oc = 1 - ic

    def dev(x=0, y=0, z=0, c=0):
        core = oc if c else ic
        return (lax.rem(ix + x, NX), lax.rem(iz + z, NZ), lax.rem(iy + y, NY) * 2 + core)

    partners = (
        [dev(x=k) for k in range(1, NX)] + [dev(y=k) for k in range(1, NY)]
        + [dev(z=k) for k in range(1, NZ)] + [dev(c=1)]
    )
    barrier = pltpu.get_barrier_semaphore()
    for p in partners:
        pl.semaphore_signal(barrier, inc=1, device_id=p, device_id_type=MESH)

    loads = []

    def load(src, dst):
        cp = pltpu.make_async_copy(src, dst, lsem.at[len(loads)])
        cp.start()
        loads.append(cp)

    load(tokens, tin)
    load(routes, rin)
    load(weights, win)
    n_w1, n_all = 3 + 8 * NX, 3 + 12 * NX

    def load_first():
        zero = jnp.zeros((SQ // 2, HALF), BF16)
        for h in range(2):
            w1[h, 3, TQ + 32:HQ] = zero
            w1[h, 3, HQ + TQ + 32:] = zero
        for j in range(NX):
            n = SQ if j < 3 else SQ // 2
            for h in range(2):
                cols = pl.ds(h * HALF, HALF)
                load(tgate.at[pl.ds(j * TQ, TQ), cols], w1.at[h, j, pl.ds(0, TQ)])
                load(sgate.at[0, pl.ds(j * SQ, n), cols], w1.at[h, j, pl.ds(TQ, n)])
                load(tup.at[pl.ds(j * TQ, TQ), cols], w1.at[h, j, pl.ds(HQ, TQ)])
                load(sup.at[0, pl.ds(j * SQ, n), cols], w1.at[h, j, pl.ds(HQ + TQ, n)])

    def load_down():
        zero = jnp.zeros((SQ // 2, HALF), BF16)
        for h in range(2):
            wd[h, 3, TQ + 32:HQ] = zero
        for j in range(NX):
            n = SQ if j < 3 else SQ // 2
            for h in range(2):
                cols = pl.ds(h * HALF, HALF)
                load(tdown.at[pl.ds(j * TQ, TQ), cols], wd.at[h, j, pl.ds(0, TQ)])
                load(sdown.at[0, pl.ds(j * SQ, n), cols], wd.at[h, j, pl.ds(TQ, n)])

    loaded = set()

    def weights_ready(first, last):
        for i in range(first, last):
            if i not in loaded:
                loaded.add(i)
                loads[i].wait()

    weights_ready(0, 3)

    for h in range(2):
        tf[h] = tin[:, h * HALF:(h + 1) * HALF].astype(F32)
    blk[pl.ds(pl.multiple_of(ic * 8, 8), 8), :] = tf[ic]
    pl.semaphore_wait(barrier, len(partners))

    sent = []

    def send(src, dst, to):
        i = len(sent)
        cp = pltpu.make_async_remote_copy(
            src_ref=src, dst_ref=dst, send_sem=ssem.at[i], recv_sem=rsem.at[i],
            device_id=to, device_id_type=MESH,
        )
        cp.start()
        sent.append(cp)
        return cp

    landed = set()

    def arrived(copies):
        for c in copies:
            if id(c) not in landed:
                landed.add(id(c))
                c.wait_recv()

    def exchange():
        cp = send(tf.at[oc], blk.at[pl.ds(pl.multiple_of(ic * 8, 8), 8), :], dev(c=1))
        cp.wait_recv()
        tok[ic, 0, 0:ROWS] = blk[...].astype(BF16)

    pcols, qcols = pl.ds(0, PC), pl.ds(PC, HALF - PC)

    def rows(k):
        return pl.ds((k % NY) * ROWS, ROWS)

    def group(part):
        return pl.ds(part * SLABS, SLABS)

    cps = {}

    def gather_tasks(buf, name):
        own = buf.at[ic, 0, pl.ds(0, ROWS)]

        def y_first():
            for key, cols in (("P1", pcols), ("PQ", qcols)):
                cps[key + name] = [
                    send(own.at[:, cols], buf.at[ic, 0, rows(-k), cols], dev(y=k)) for k in (2, 1, 3)
                ]

        def z_first(part):
            cps["Q1" + name, part] = [
                send(own.at[:, qcols], buf.at[ic, POS[-k % NZ], pl.ds(0, ROWS), qcols], dev(z=k)) for k in ZSEND[part]
            ]

        def y_then_z(part):
            arrived(cps.pop("P1" + name, []))
            cps["P2" + name, part] = [
                send(buf.at[ic, 0, :, pcols], buf.at[ic, POS[-k % NZ], :, pcols], dev(z=k)) for k in ZSEND[part]
            ]

        def z_then_y(part):
            arrived(cps["Q1" + name, part])
            g = group(part) if part else pl.ds(1, SLABS - 1)
            cps["S" + name, part] = [
                send(buf.at[ic, g, pl.ds(0, ROWS), qcols], buf.at[ic, g, rows(-k), qcols], dev(y=k)) for k in (2, 1, 3)
            ]

        def to_core(part):
            arrived(cps["P2" + name, part])
            arrived(cps["S" + name, part])
            if part == 0:
                arrived(cps["PQ" + name])
            cps["K" + name, part] = [send(buf.at[ic, group(part)], buf.at[ic, group(part)], dev(c=1))]

        return {"P1": y_first, "Q1": z_first, "P2": y_then_z, "S": z_then_y, "K": to_core}

    def piece(buf, h, part):
        return buf[h, part * SLABS:(part + 1) * SLABS].reshape(CHUNK, HALF)

    def own_half(part):
        weights_ready(3, n_w1)
        arrived(cps["P2A", part])
        arrived(cps["SA", part])
        if part == 0:
            arrived(cps["PQA"])
        for d in range(NX):
            bacc[part, d] = dot(w1[ic, lax.rem(ix + d, NX)], piece(tok, ic, part), NT)

    def hidden_parts(part):
        arrived(cps["KA", part])
        out = []
        for d in (2, 1, 3, 0):
            val = bacc[part, d] + dot(w1[oc, lax.rem(ix + d, NX)], piece(tok, oc, part), NT)
            if d == 0 or (RELAY[part] and d != 2):
                bacc[part, d] = val
                continue
            psend[part, d] = val.astype(BF16)
            if RELAY[part]:
                cps["R", part] = [
                    send(psend.at[part, d, pl.ds(0, HQ)], pass_on.at[part, 0], dev(x=1)),
                    send(psend.at[part, d, pl.ds(HQ, HQ)], pass_on.at[part, 1], dev(x=3)),
                ]
            else:
                out.append(send(psend.at[part, d], prec.at[part, NX - d], dev(x=d)))
        cps["B", part] = out

    def relay(part):
        arrived(cps["R", part])
        for n, d in enumerate((1, 3)):
            mid = slice(n * HQ, n * HQ + HQ)
            rest = slice(HQ - n * HQ, 2 * HQ - n * HQ)
            psend[part, d, mid] = (bacc[part, d, mid] + pass_on[part, n].astype(F32)).astype(BF16)
            psend[part, d, rest] = bacc[part, d, rest].astype(BF16)
            cps["B", part].append(send(psend.at[part, d], prec.at[part, NX - d], dev(x=d)))

    def activate(part):
        arrived(cps["B", part])
        total = bacc[part, 0]
        for d in (1, 3) if RELAY[part] else (1, 2, 3):
            total = total + prec[part, d].astype(F32)
        pre, lift = total[:HQ], total[HQ:]
        s = jax.nn.sigmoid(pre)
        act = pre * s
        hidden = act * lift
        weight = mix[part, 0:1]
        hall[part, ix, 0:TQ] = (-hidden[:TQ]).astype(BF16)
        hall[part, ix, TQ:HQ] = (hidden[TQ:] * weight).astype(BF16)
        mine = hall.at[part, ix]
        cps["A", part] = [send(mine, mine, dev(x=d)) for d in ((1, 3) if DRELAY[part] else (2, 1, 3))]
        slope = s * (1.0 + pre * (1.0 - s))
        fac[ix, part, 0] = (weight * (lift * slope)[TQ:]).astype(BF16)
        fac[ix, part, 1] = (weight * act[TQ:]).astype(BF16)

    def factors():
        cps["FAC"] = [send(fac.at[ix], fac.at[ix], dev(x=k)) for k in (2, 1, 3)]

    def pass_hidden(part):
        arrived(cps["A", part])
        cps["DR", part] = []
        for d, first, n in ((1, 0, 96), (3, 96, HQ - 96)):
            piece_of = hall.at[part, lax.rem(ix + NX - d, NX), pl.ds(first, n)]
            cps["DR", part].append(send(piece_of, piece_of, dev(x=d)))

    def outputs(part):
        weights_ready(n_w1, n_all)
        arrived(cps["A", part])
        arrived(cps.get(("DR", part), []))
        hidden = hall[part].reshape(NX * HQ, CHUNK).T
        fcore[part] = dot(hidden, wd[oc].reshape(NX * HQ, HALF)).astype(BF16)
        cps["E", part] = [send(fcore.at[part], rcore.at[part], dev(c=1))]
        facc[part] = dot(hidden, wd[ic].reshape(NX * HQ, HALF))

    def scatter_first(part):
        arrived(cps["E", part])
        total = facc[part] + rcore[part].astype(F32)
        facc[part] = total
        fsend[part * SLABS:(part + 1) * SLABS] = total.astype(BF16).reshape(SLABS, 64, HALF)
        cps["F1", part] = [
            send(fsend.at[group(part), rows(k), qcols], ry.at[part, NY - k], dev(y=k)) for k in (2, 1, 3)
        ]
        cps["F1P", part] = [
            send(fsend.at[pos, :, pcols], rz.at[POS[-ORDER[pos] % NZ]], dev(z=ORDER[pos]))
            for pos in range(part * SLABS, (part + 1) * SLABS) if ORDER[pos]
        ]

    def scatter_second(part):
        arrived(cps["F1", part])
        total = facc[part].reshape(SLABS, 64, HALF)[:, :ROWS, PC:]
        for d in range(1, NY):
            total = total + ry[part, d].astype(F32)
        if part == 0:
            ysend[0:ROWS, PC:] = total[0]
        qsend[part * SLABS:(part + 1) * SLABS] = total.astype(BF16)
        cps["F2", part] = [
            send(qsend.at[pos], rqz.at[POS[-ORDER[pos] % NZ]], dev(z=ORDER[pos]))
            for pos in range(part * SLABS, (part + 1) * SLABS) if ORDER[pos]
        ]

    def scatter_y():
        total = facc[0, 0:64, :PC]
        for part in range(PARTS):
            arrived(cps["F1P", part])
        for pos in range(1, NZ):
            total = total + rz[pos].astype(F32)
        ysend[:, :PC] = total
        rpy[0] = total.astype(BF16)
        cps["FP"] = [send(rpy.at[0, rows(k)], rpy.at[NY - k, pl.ds(0, ROWS)], dev(y=k)) for k in (2, 1, 3)]

    def residual_q():
        for part in range(PARTS):
            arrived(cps["F2", part])
        total = ysend[0:ROWS, PC:]
        for pos in range(1, NZ):
            total = total + rqz[pos].astype(F32)
        res[ic, 0, 0:ROWS, PC:] = total.astype(BF16)

    def residual_p():
        arrived(cps["FP"])
        total = ysend[0:ROWS, :PC]
        for k in range(1, NY):
            total = total + rpy[k, 0:ROWS].astype(F32)
        res[ic, 0, 0:ROWS, :PC] = total.astype(BF16)

    def mixing():
        m = jnp.sum(jnp.where(rin[...] == ie, win[...], 0.0), axis=0, keepdims=True)
        m = jnp.broadcast_to(m, (8, TOKENS))
        m = pltpu.roll(m, lax.rem(NZ - iz, NZ) * 64, 1)
        lane = lax.broadcasted_iota(jnp.int32, (8, TOKENS), 1)
        near = pltpu.roll(m, lax.rem(TOKENS - iy * ROWS, TOKENS), 1)
        far = pltpu.roll(m, 64 - iy * ROWS, 1)
        m = jnp.where(lax.rem(lane, 64) < 64 - iy * ROWS, near, far)
        low = lax.broadcasted_iota(jnp.int32, (8, CHUNK), 1) < 64
        for part in range(PARTS):
            two = []
            for side in range(2):
                k = ORDER[part * 2 + side]
                t = m[:, (k // 2) * CHUNK:(k // 2 + 1) * CHUNK]
                two.append(t if k % 2 == side else pltpu.roll(t, 64, 1))
            mix[part] = jnp.where(low, two[0], two[1])

    def hidden_grads(part):
        arrived(cps["KG", part])
        left = [wd[h, :, TQ:].reshape(NX * SQ, HALF) for h in range(2)]
        val = dot(left[0], piece(res, 0, part), NT) + dot(left[1], piece(res, 1, part), NT)
        iown[part] = val.reshape(NX, SQ, CHUNK)
        isend[part] = val.astype(BF16).reshape(NX, SQ, CHUNK)
        if DIRECT[part]:
            out = [send(isend.at[part], iall.at[part, NX - d], dev(x=d)) for d in (2, 1, 3)]
        else:
            out = [
                send(isend.at[part, lax.rem(ix + d, NX)], irec.at[part, NX - d], dev(x=d)) for d in (2, 1, 3)
            ]
        cps["H", part] = out

    def hidden_sum(part):
        arrived(cps["H", part])
        total = iown[part, ix]
        for d in range(1, NX):
            total = total + irec[part, d].astype(F32)
        hgrad[part, ix] = total.astype(BF16)
        mine = hgrad.at[part, ix]
        cps["HS", part] = [send(mine, mine, dev(x=d)) for d in (2, 1, 3)]

    def slopes(part):
        arrived(cps["H" if DIRECT[part] else "HS", part])
        arrived(cps["FAC"])
        cols = pl.ds(part * CHUNK, CHUNK)
        if DIRECT[part]:
            grad = iown[part].reshape(NX * SQ, CHUNK)
            for d in range(1, NX):
                grad = grad + iall[part, d].reshape(NX * SQ, CHUNK).astype(F32)
            pgrad[:, cols] = (grad * fac[:, part, 0].reshape(NX * SQ, CHUNK).astype(F32)).astype(BF16)
            lgrad[:, cols] = (grad * fac[:, part, 1].reshape(NX * SQ, CHUNK).astype(F32)).astype(BF16)
            return
        for j in range(NX):
            grad = hgrad[part, j].astype(F32)
            units = pl.ds(j * SQ, SQ)
            pgrad[units, cols] = (grad * fac[j, part, 0].astype(F32)).astype(BF16)
            lgrad[units, cols] = (grad * fac[j, part, 1].astype(F32)).astype(BF16)

    def weighted_hidden():
        for part in range(PARTS):
            for j in range(NX):
                hm[j * SQ:(j + 1) * SQ, part * CHUNK:(part + 1) * CHUNK] = hall[part, j, TQ:HQ]

    def down_product():
        for h in range(2):
            gd[h] = dot(hm[:STUD], res[h].reshape(TOKENS, HALF)).astype(BF16)

    tasks = {
        "X0": exchange, "MIX": mixing, "HM": weighted_hidden, "FAC": factors,
        "LD1": load_first, "LD2": load_down, "DR": pass_hidden, "GD": down_product,
        "O": own_half, "B": hidden_parts, "R": relay, "A": activate, "E": outputs, "F1": scatter_first,
        "F2": scatter_second, "FP": scatter_y, "FQ": residual_q, "FF": residual_p, "H": hidden_grads,
        "HS": hidden_sum, "SL": slopes,
    }
    for name, buf in (("A", tok), ("G", res)):
        tasks.update({key + name: task for key, task in gather_tasks(buf, name).items()})
    for step in ("".join(PROGRAM)).split():
        key, _, part = step.partition(".")
        tasks[key](*([int(part)] if part else []))
    for cp in sent:
        cp.wait_send()


def products(tok, gd, pgrad, lgrad, ggate, gup, gdown, stage, sem):
    copies = []

    def write(src, out, n, h):
        cp = pltpu.make_async_copy(src, out.at[0, :, pl.ds(h * HALF, HALF)], sem.at[n, h])
        cp.start()
        copies.append(cp)

    for h in range(2):
        write(gd.at[h], gdown, 2, h)
    for n, (left, out) in enumerate(((pgrad, ggate), (lgrad, gup))):
        for h in range(2):
            stage[n, h] = dot(left[:STUD], tok[h].reshape(TOKENS, HALF)).astype(BF16)
            write(stage.at[n, h], out, n, h)
    for cp in copies:
        cp.wait()


def body(tokens, tgate, tup, tdown, sgate, sup, sdown, routes, route_weight):
    vmem, anym = pl.BlockSpec(memory_space=pltpu.VMEM), pl.BlockSpec(memory_space=pl.ANY)
    V = pltpu.VMEM
    held = (
        V((2, NZ, 64, HALF), BF16),
        V((2, STUD, HALF), BF16),
        V((NX * SQ, TOKENS), BF16),
        V((NX * SQ, TOKENS), BF16),
    )
    args = (tokens, routes.T, route_weight.T, tgate, tup, tdown, sgate, sup, sdown)
    parts = pl.pallas_call(
        kernel,
        out_shape=held,
        in_specs=[anym] * 9,
        out_specs=(vmem,) * 4,
        scratch_shapes=[
            V((2, NZ, 64, HALF), BF16),
            V((NX * SQ, TOKENS), BF16),
            V((8, WIDTH), BF16),
            V((2, TOKENS), jnp.int32),
            V((2, TOKENS), F32),
            V((2, NX, 2 * HQ, HALF), BF16),
            V((2, NX, HQ, HALF), BF16),
            V((2, 8, HALF), F32),
            V((ROWS, HALF), F32),
            V((PARTS, 8, CHUNK), F32),
            V((PARTS, NX, 2 * HQ, CHUNK), F32),
            V((PARTS, NX, 2 * HQ, CHUNK), BF16),
            V((PARTS, NX, 2 * HQ, CHUNK), BF16),
            V((PARTS, 2, HQ, CHUNK), BF16),
            V((PARTS, NX, HQ, CHUNK), BF16),
            V((NX, PARTS, 2, SQ, CHUNK), BF16),
            V((PARTS, CHUNK, HALF), BF16),
            V((PARTS, CHUNK, HALF), BF16),
            V((PARTS, CHUNK, HALF), F32),
            V((NZ, 64, HALF), BF16),
            V((NZ, 64, PC), BF16),
            V((PARTS, NY, SLABS, ROWS, HALF - PC), BF16),
            V((NZ, ROWS, HALF - PC), BF16),
            V((NZ, ROWS, HALF - PC), BF16),
            V((64, HALF), F32),
            V((NY, 64, PC), BF16),
            V((PARTS, NX, SQ, CHUNK), BF16),
            V((PARTS, NX, SQ, CHUNK), BF16),
            V((PARTS, NX, NX, SQ, CHUNK), BF16),
            V((PARTS, NX, SQ, CHUNK), F32),
            V((PARTS, NX, SQ, CHUNK), BF16),
            pltpu.SemaphoreType.DMA((64,)),
            pltpu.SemaphoreType.DMA((NSEM,)),
            pltpu.SemaphoreType.DMA((NSEM,)),
        ],
        compiler_params=pltpu.CompilerParams(
            collective_id=0, has_side_effects=True, vmem_limit_bytes=40 * 2**20
        ),
        cost_estimate=pl.CostEstimate(flops=6 * 10**9, bytes_accessed=12 * 10**6, transcendentals=10**6),
        name="distill",
    )(*(pltpu.with_memory_space_constraint(a, pltpu.HBM) for a in args))
    grad = jax.ShapeDtypeStruct((1, STUD, WIDTH), BF16)
    return pl.pallas_call(
        products,
        out_shape=(grad, grad, grad),
        in_specs=[vmem] * 4,
        out_specs=(anym,) * 3,
        scratch_shapes=[V((2, 2, STUD, HALF), BF16), pltpu.SemaphoreType.DMA((3, 2))],
        compiler_params=pltpu.CompilerParams(vmem_limit_bytes=16 * 2**20),
        cost_estimate=pl.CostEstimate(flops=15 * 10**8, bytes_accessed=3 * 10**6, transcendentals=0),
        name="products",
    )(*parts)


def solution(mesh):
    split = P(("neuron", "expert"), "dp")
    expert = P("expert", "neuron", "dp")
    return jax.shard_map(
        body,
        mesh=mesh,
        in_specs=(split, split, split, split, expert, expert, expert, P(), P()),
        out_specs=(expert, expert, expert),
        check_vma=False,
    )
```

```python
import jax
import jax.numpy as jnp
from jax import lax
from jax.experimental import pallas as pl
from jax.experimental.pallas import tpu as pltpu
from jax.sharding import PartitionSpec as P

MESH = pl.DeviceIdType.MESH
F32, BF16 = jnp.float32, jnp.bfloat16
NX, NY, NZ = 4, 4, 8
ROWS = 16
WIDTH, HALF = 2048, 1024
TEACH, STUD = 448, 224
TQ, SQ = 112, 64
HQ = TQ + SQ
CHUNK, PARTS, SLABS = 128, 4, 2
TOKENS = CHUNK * PARTS
ORDER = (0, 1, 7, 2, 6, 3, 5, 4)
POS = tuple(ORDER.index(k) for k in range(NZ))
PC = 256
ZSEND = ((7,), (1, 6), (2, 5), (3, 4))
NSEM = 192
DRELAY = (0, 0, 0, 0)
DIRECT = (0, 0, 1, 1)
RELAY = (1, 1, 1, 1)
NT = (((1,), (1,)), ((), ()))


PROGRAM = (
    "X0 Q1A.0 Q1A.2 P1A ",
    "Q1A.3 MIX Q1A.1 LD1 ",
    "SA.0 P2A.0 P2A.2 P2A.3 ",
    "SA.2 KA.0 SA.3 P2A.1 ",
    "SA.1 O.0 B.0 KA.2 ",
    "O.2 B.2 KA.3 R.0 ",
    "KA.1 O.3 B.3 R.2 ",
    "O.1 B.1 LD2 R.3 ",
    "A.2 R.1 A.3 E.2 ",
    "A.1 A.0 E.3 F1.2 ",
    "F1.3 E.1 E.0 F1.1 ",
    "F1.0 F2.3 F2.2 F2.1 ",
    "FP FAC F2.0 WS ",
    "FQ Q1G.0 FF P1G ",
    "Q1G.1 Q1G.2 Q1G.3 WS ",
    "SG.0 P2G.0 P2G.1 SG.1 ",
    "P2G.2 P2G.3 SG.2 KG.0 ",
    "HO.0 H.0 SG.3 KG.1 ",
    "HO.1 KG.2 HO.2 H.1 ",
    "HS.0 H.2 KG.3 HO.3 ",
    "HS.1 H.3 HM WS ",
    "SL.1 SL.0 GD SL.2 ",
    "SL.3 ",
)


def dot(a, b, dims=(((1,), (0,)), ((), ()))):
    return lax.dot_general(a, b, dims, preferred_element_type=F32)


def kernel(
    tokens, routes, weights, tgate, tup, tdown, sgate, sup, sdown,
    tok, gd, pgrad, lgrad,
    res, hm, tin, rin, win, w1, wd, tf, blk, mix, bacc, psend, prec, pass_on, hall, fac,
    fcore, rcore, facc, fsend, rz, ry, qsend, rqz, ysend, rpy,
    isend, irec, iall, iown, hgrad, lsem, ssem, rsem,
):
    ix, iz, ie = lax.axis_index("dp"), lax.axis_index("neuron"), lax.axis_index("expert")
    iy, ic = ie // 2, lax.rem(ie, 2)
    oc = 1 - ic

    def dev(x=0, y=0, z=0, c=0):
        core = oc if c else ic
        return (lax.rem(ix + x, NX), lax.rem(iz + z, NZ), lax.rem(iy + y, NY) * 2 + core)

    partners = (
        [dev(x=k) for k in range(1, NX)] + [dev(y=k) for k in range(1, NY)]
        + [dev(z=k) for k in range(1, NZ)] + [dev(c=1)]
    )
    barrier = pltpu.get_barrier_semaphore()
    for p in partners:
        pl.semaphore_signal(barrier, inc=1, device_id=p, device_id_type=MESH)

    loads = []

    def load(src, dst):
        cp = pltpu.make_async_copy(src, dst, lsem.at[len(loads)])
        cp.start()
        loads.append(cp)

    load(tokens, tin)
    load(routes, rin)
    load(weights, win)
    n_w1, n_all = 3 + 8 * NX, 3 + 12 * NX

    def load_first():
        zero = jnp.zeros((SQ // 2, HALF), BF16)
        for h in range(2):
            w1[h, 3, TQ + 32:HQ] = zero
            w1[h, 3, HQ + TQ + 32:] = zero
        for j in range(NX):
            n = SQ if j < 3 else SQ // 2
            for h in range(2):
                cols = pl.ds(h * HALF, HALF)
                load(tgate.at[pl.ds(j * TQ, TQ), cols], w1.at[h, j, pl.ds(0, TQ)])
                load(sgate.at[0, pl.ds(j * SQ, n), cols], w1.at[h, j, pl.ds(TQ, n)])
                load(tup.at[pl.ds(j * TQ, TQ), cols], w1.at[h, j, pl.ds(HQ, TQ)])
                load(sup.at[0, pl.ds(j * SQ, n), cols], w1.at[h, j, pl.ds(HQ + TQ, n)])

    def load_down():
        zero = jnp.zeros((SQ // 2, HALF), BF16)
        for h in range(2):
            wd[h, 3, TQ + 32:HQ] = zero
        for j in range(NX):
            n = SQ if j < 3 else SQ // 2
            for h in range(2):
                cols = pl.ds(h * HALF, HALF)
                load(tdown.at[pl.ds(j * TQ, TQ), cols], wd.at[h, j, pl.ds(0, TQ)])
                load(sdown.at[0, pl.ds(j * SQ, n), cols], wd.at[h, j, pl.ds(TQ, n)])

    loaded = set()

    def weights_ready(first, last):
        for i in range(first, last):
            if i not in loaded:
                loaded.add(i)
                loads[i].wait()

    weights_ready(0, 3)

    for h in range(2):
        tf[h] = tin[:, h * HALF:(h + 1) * HALF].astype(F32)
    blk[pl.ds(pl.multiple_of(ic * 8, 8), 8), :] = tf[ic]
    pl.semaphore_wait(barrier, len(partners))

    sent = []

    def send(src, dst, to):
        i = len(sent)
        cp = pltpu.make_async_remote_copy(
            src_ref=src, dst_ref=dst, send_sem=ssem.at[i], recv_sem=rsem.at[i],
            device_id=to, device_id_type=MESH,
        )
        cp.start()
        sent.append(cp)
        return cp

    landed = set()

    left_off = [0]

    def finish(spare):
        last = max(len(sent) - spare, left_off[0])
        for cp in sent[left_off[0]:last]:
            cp.wait_send()
        left_off[0] = last

    def arrived(copies):
        for c in copies:
            if id(c) not in landed:
                landed.add(id(c))
                c.wait_recv()

    def exchange():
        cp = send(tf.at[oc], blk.at[pl.ds(pl.multiple_of(ic * 8, 8), 8), :], dev(c=1))
        cp.wait_recv()
        tok[ic, 0, 0:ROWS] = blk[...].astype(BF16)

    pcols, qcols = pl.ds(0, PC), pl.ds(PC, HALF - PC)

    def rows(k):
        return pl.ds((k % NY) * ROWS, ROWS)

    def group(part):
        return pl.ds(part * SLABS, SLABS)

    cps = {}

    def gather_tasks(buf, name):
        own = buf.at[ic, 0, pl.ds(0, ROWS)]

        def y_first():
            for key, cols in (("P1", pcols), ("PQ", qcols)):
                cps[key + name] = [
                    send(own.at[:, cols], buf.at[ic, 0, rows(-k), cols], dev(y=k)) for k in (2, 1, 3)
                ]

        def z_first(part):
            cps["Q1" + name, part] = [
                send(own.at[:, qcols], buf.at[ic, POS[-k % NZ], pl.ds(0, ROWS), qcols], dev(z=k)) for k in ZSEND[part]
            ]

        def y_then_z(part):
            arrived(cps.pop("P1" + name, []))
            cps["P2" + name, part] = [
                send(buf.at[ic, 0, :, pcols], buf.at[ic, POS[-k % NZ], :, pcols], dev(z=k)) for k in ZSEND[part]
            ]

        def z_then_y(part):
            arrived(cps["Q1" + name, part])
            g = group(part) if part else pl.ds(1, SLABS - 1)
            cps["S" + name, part] = [
                send(buf.at[ic, g, pl.ds(0, ROWS), qcols], buf.at[ic, g, rows(-k), qcols], dev(y=k)) for k in (2, 1, 3)
            ]

        def to_core(part):
            arrived(cps["P2" + name, part])
            arrived(cps["S" + name, part])
            if part == 0:
                arrived(cps["PQ" + name])
            cps["K" + name, part] = [send(buf.at[ic, group(part)], buf.at[ic, group(part)], dev(c=1))]

        return {"P1": y_first, "Q1": z_first, "P2": y_then_z, "S": z_then_y, "K": to_core}

    def piece(buf, h, part):
        return buf[h, part * SLABS:(part + 1) * SLABS].reshape(CHUNK, HALF)

    def own_half(part):
        weights_ready(3, n_w1)
        arrived(cps["P2A", part])
        arrived(cps["SA", part])
        if part == 0:
            arrived(cps["PQA"])
        for d in range(NX):
            bacc[part, d] = dot(w1[ic, lax.rem(ix + d, NX)], piece(tok, ic, part), NT)

    def hidden_parts(part):
        arrived(cps["KA", part])
        out = []
        for d in (2, 1, 3, 0):
            val = bacc[part, d] + dot(w1[oc, lax.rem(ix + d, NX)], piece(tok, oc, part), NT)
            if d == 0 or (RELAY[part] and d != 2):
                bacc[part, d] = val
                continue
            psend[part, d] = val.astype(BF16)
            if RELAY[part]:
                cps["R", part] = [
                    send(psend.at[part, d, pl.ds(0, HQ)], pass_on.at[part, 0], dev(x=1)),
                    send(psend.at[part, d, pl.ds(HQ, HQ)], pass_on.at[part, 1], dev(x=3)),
                ]
            else:
                out.append(send(psend.at[part, d], prec.at[part, NX - d], dev(x=d)))
        cps["B", part] = out

    def relay(part):
        arrived(cps["R", part])
        for n, d in enumerate((1, 3)):
            mid = slice(n * HQ, n * HQ + HQ)
            rest = slice(HQ - n * HQ, 2 * HQ - n * HQ)
            psend[part, d, mid] = (bacc[part, d, mid] + pass_on[part, n].astype(F32)).astype(BF16)
            psend[part, d, rest] = bacc[part, d, rest].astype(BF16)
            cps["B", part].append(send(psend.at[part, d], prec.at[part, NX - d], dev(x=d)))

    def activate(part):
        arrived(cps["B", part])
        total = bacc[part, 0]
        for d in (1, 3) if RELAY[part] else (1, 2, 3):
            total = total + prec[part, d].astype(F32)
        pre, lift = total[:HQ], total[HQ:]
        s = jax.nn.sigmoid(pre)
        act = pre * s
        hidden = act * lift
        weight = mix[part, 0:1]
        hall[part, ix, 0:TQ] = (-hidden[:TQ]).astype(BF16)
        hall[part, ix, TQ:HQ] = (hidden[TQ:] * weight).astype(BF16)
        mine = hall.at[part, ix]
        cps["A", part] = [send(mine, mine, dev(x=d)) for d in ((1, 3) if DRELAY[part] else (2, 1, 3))]
        slope = s * (1.0 + pre * (1.0 - s))
        fac[ix, part, 0] = (weight * (lift * slope)[TQ:]).astype(BF16)
        fac[ix, part, 1] = (weight * act[TQ:]).astype(BF16)

    def factors():
        cps["FAC"] = [send(fac.at[ix], fac.at[ix], dev(x=k)) for k in (2, 1, 3)]

    def pass_hidden(part):
        arrived(cps["A", part])
        cps["DR", part] = []
        for d, first, n in ((1, 0, 96), (3, 96, HQ - 96)):
            piece_of = hall.at[part, lax.rem(ix + NX - d, NX), pl.ds(first, n)]
            cps["DR", part].append(send(piece_of, piece_of, dev(x=d)))

    def outputs(part):
        weights_ready(n_w1, n_all)
        arrived(cps["A", part])
        arrived(cps.get(("DR", part), []))
        hidden = hall[part].reshape(NX * HQ, CHUNK).T
        fcore[part] = dot(hidden, wd[oc].reshape(NX * HQ, HALF)).astype(BF16)
        cps["E", part] = [send(fcore.at[part], rcore.at[part], dev(c=1))]
        facc[part] = dot(hidden, wd[ic].reshape(NX * HQ, HALF))

    def scatter_first(part):
        arrived(cps["E", part])
        total = facc[part] + rcore[part].astype(F32)
        facc[part] = total
        fsend[part * SLABS:(part + 1) * SLABS] = total.astype(BF16).reshape(SLABS, 64, HALF)
        cps["F1", part] = [
            send(fsend.at[group(part), rows(k), qcols], ry.at[part, NY - k], dev(y=k)) for k in (2, 1, 3)
        ]
        cps["F1P", part] = [
            send(fsend.at[pos, :, pcols], rz.at[POS[-ORDER[pos] % NZ]], dev(z=ORDER[pos]))
            for pos in range(part * SLABS, (part + 1) * SLABS) if ORDER[pos]
        ]

    def scatter_second(part):
        arrived(cps["F1", part])
        total = facc[part].reshape(SLABS, 64, HALF)[:, :ROWS, PC:]
        for d in range(1, NY):
            total = total + ry[part, d].astype(F32)
        if part == 0:
            ysend[0:ROWS, PC:] = total[0]
        qsend[part * SLABS:(part + 1) * SLABS] = total.astype(BF16)
        cps["F2", part] = [
            send(qsend.at[pos], rqz.at[POS[-ORDER[pos] % NZ]], dev(z=ORDER[pos]))
            for pos in range(part * SLABS, (part + 1) * SLABS) if ORDER[pos]
        ]

    def scatter_y():
        total = facc[0, 0:64, :PC]
        for part in range(PARTS):
            arrived(cps["F1P", part])
        for pos in range(1, NZ):
            total = total + rz[pos].astype(F32)
        ysend[:, :PC] = total
        rpy[0] = total.astype(BF16)
        cps["FP"] = [send(rpy.at[0, rows(k)], rpy.at[NY - k, pl.ds(0, ROWS)], dev(y=k)) for k in (2, 1, 3)]

    def residual_q():
        for part in range(PARTS):
            arrived(cps["F2", part])
        total = ysend[0:ROWS, PC:]
        for pos in range(1, NZ):
            total = total + rqz[pos].astype(F32)
        res[ic, 0, 0:ROWS, PC:] = total.astype(BF16)

    def residual_p():
        arrived(cps["FP"])
        total = ysend[0:ROWS, :PC]
        for k in range(1, NY):
            total = total + rpy[k, 0:ROWS].astype(F32)
        res[ic, 0, 0:ROWS, :PC] = total.astype(BF16)

    def mixing():
        m = jnp.sum(jnp.where(rin[...] == ie, win[...], 0.0), axis=0, keepdims=True)
        m = jnp.broadcast_to(m, (8, TOKENS))
        m = pltpu.roll(m, lax.rem(NZ - iz, NZ) * 64, 1)
        lane = lax.broadcasted_iota(jnp.int32, (8, TOKENS), 1)
        near = pltpu.roll(m, lax.rem(TOKENS - iy * ROWS, TOKENS), 1)
        far = pltpu.roll(m, 64 - iy * ROWS, 1)
        m = jnp.where(lax.rem(lane, 64) < 64 - iy * ROWS, near, far)
        low = lax.broadcasted_iota(jnp.int32, (8, CHUNK), 1) < 64
        for part in range(PARTS):
            two = []
            for side in range(2):
                k = ORDER[part * 2 + side]
                t = m[:, (k // 2) * CHUNK:(k // 2 + 1) * CHUNK]
                two.append(t if k % 2 == side else pltpu.roll(t, 64, 1))
            mix[part] = jnp.where(low, two[0], two[1])

    def own_hidden_grads(part):
        left = wd[ic, :, TQ:].reshape(NX * SQ, HALF)
        iown[part] = dot(left, piece(res, ic, part), NT).reshape(NX, SQ, CHUNK)

    def hidden_grads(part):
        arrived(cps["KG", part])
        left = wd[oc, :, TQ:].reshape(NX * SQ, HALF)
        val = iown[part].reshape(NX * SQ, CHUNK) + dot(left, piece(res, oc, part), NT)
        iown[part] = val.reshape(NX, SQ, CHUNK)
        isend[part] = val.astype(BF16).reshape(NX, SQ, CHUNK)
        if DIRECT[part]:
            out = [send(isend.at[part], iall.at[part, NX - d], dev(x=d)) for d in (2, 1, 3)]
        else:
            out = [
                send(isend.at[part, lax.rem(ix + d, NX)], irec.at[part, NX - d], dev(x=d)) for d in (2, 1, 3)
            ]
        cps["H", part] = out

    def hidden_sum(part):
        arrived(cps["H", part])
        total = iown[part, ix]
        for d in range(1, NX):
            total = total + irec[part, d].astype(F32)
        hgrad[part, ix] = total.astype(BF16)
        mine = hgrad.at[part, ix]
        cps["HS", part] = [send(mine, mine, dev(x=d)) for d in (2, 1, 3)]

    def slopes(part):
        arrived(cps["H" if DIRECT[part] else "HS", part])
        arrived(cps["FAC"])
        cols = pl.ds(part * CHUNK, CHUNK)
        if DIRECT[part]:
            grad = iown[part].reshape(NX * SQ, CHUNK)
            for d in range(1, NX):
                grad = grad + iall[part, d].reshape(NX * SQ, CHUNK).astype(F32)
            pgrad[:, cols] = (grad * fac[:, part, 0].reshape(NX * SQ, CHUNK).astype(F32)).astype(BF16)
            lgrad[:, cols] = (grad * fac[:, part, 1].reshape(NX * SQ, CHUNK).astype(F32)).astype(BF16)
            return
        for j in range(NX):
            grad = hgrad[part, j].astype(F32)
            units = pl.ds(j * SQ, SQ)
            pgrad[units, cols] = (grad * fac[j, part, 0].astype(F32)).astype(BF16)
            lgrad[units, cols] = (grad * fac[j, part, 1].astype(F32)).astype(BF16)

    def weighted_hidden():
        for part in range(PARTS):
            for j in range(NX):
                hm[j * SQ:(j + 1) * SQ, part * CHUNK:(part + 1) * CHUNK] = hall[part, j, TQ:HQ]

    def down_product():
        for h in range(2):
            gd[h] = dot(hm[:STUD], res[h].reshape(TOKENS, HALF)).astype(BF16)

    tasks = {
        "X0": exchange, "MIX": mixing, "HM": weighted_hidden, "FAC": factors,
        "WS": lambda: finish(12), "LD1": load_first, "LD2": load_down, "DR": pass_hidden, "GD": down_product,
        "O": own_half, "B": hidden_parts, "R": relay, "A": activate, "E": outputs, "F1": scatter_first,
        "F2": scatter_second, "FP": scatter_y, "FQ": residual_q, "FF": residual_p, "HO": own_hidden_grads, "H": hidden_grads,
        "HS": hidden_sum, "SL": slopes,
    }
    for name, buf in (("A", tok), ("G", res)):
        tasks.update({key + name: task for key, task in gather_tasks(buf, name).items()})
    for step in ("".join(PROGRAM)).split():
        key, _, part = step.partition(".")
        tasks[key](*([int(part)] if part else []))
    finish(0)


def products(tok, gd, pgrad, lgrad, ggate, gup, gdown, stage, sem):
    copies = []

    def write(src, out, n, h):
        cp = pltpu.make_async_copy(src, out.at[0, :, pl.ds(h * HALF, HALF)], sem.at[n, h])
        cp.start()
        copies.append(cp)

    for h in range(2):
        write(gd.at[h], gdown, 2, h)
    for n, (left, out) in enumerate(((pgrad, ggate), (lgrad, gup))):
        for h in range(2):
            stage[n, h] = dot(left[:STUD], tok[h].reshape(TOKENS, HALF)).astype(BF16)
            write(stage.at[n, h], out, n, h)
    for cp in copies:
        cp.wait()


def body(tokens, tgate, tup, tdown, sgate, sup, sdown, routes, route_weight):
    vmem, anym = pl.BlockSpec(memory_space=pltpu.VMEM), pl.BlockSpec(memory_space=pl.ANY)
    V = pltpu.VMEM
    held = (
        V((2, NZ, 64, HALF), BF16),
        V((2, STUD, HALF), BF16),
        V((NX * SQ, TOKENS), BF16),
        V((NX * SQ, TOKENS), BF16),
    )
    args = (tokens, routes.T, route_weight.T, tgate, tup, tdown, sgate, sup, sdown)
    parts = pl.pallas_call(
        kernel,
        out_shape=held,
        in_specs=[anym] * 9,
        out_specs=(vmem,) * 4,
        scratch_shapes=[
            V((2, NZ, 64, HALF), BF16),
            V((NX * SQ, TOKENS), BF16),
            V((8, WIDTH), BF16),
            V((2, TOKENS), jnp.int32),
            V((2, TOKENS), F32),
            V((2, NX, 2 * HQ, HALF), BF16),
            V((2, NX, HQ, HALF), BF16),
            V((2, 8, HALF), F32),
            V((ROWS, HALF), F32),
            V((PARTS, 8, CHUNK), F32),
            V((PARTS, NX, 2 * HQ, CHUNK), F32),
            V((PARTS, NX, 2 * HQ, CHUNK), BF16),
            V((PARTS, NX, 2 * HQ, CHUNK), BF16),
            V((PARTS, 2, HQ, CHUNK), BF16),
            V((PARTS, NX, HQ, CHUNK), BF16),
            V((NX, PARTS, 2, SQ, CHUNK), BF16),
            V((PARTS, CHUNK, HALF), BF16),
            V((PARTS, CHUNK, HALF), BF16),
            V((PARTS, CHUNK, HALF), F32),
            V((NZ, 64, HALF), BF16),
            V((NZ, 64, PC), BF16),
            V((PARTS, NY, SLABS, ROWS, HALF - PC), BF16),
            V((NZ, ROWS, HALF - PC), BF16),
            V((NZ, ROWS, HALF - PC), BF16),
            V((64, HALF), F32),
            V((NY, 64, PC), BF16),
            V((PARTS, NX, SQ, CHUNK), BF16),
            V((PARTS, NX, SQ, CHUNK), BF16),
            V((PARTS, NX, NX, SQ, CHUNK), BF16),
            V((PARTS, NX, SQ, CHUNK), F32),
            V((PARTS, NX, SQ, CHUNK), BF16),
            pltpu.SemaphoreType.DMA((64,)),
            pltpu.SemaphoreType.DMA((NSEM,)),
            pltpu.SemaphoreType.DMA((NSEM,)),
        ],
        compiler_params=pltpu.CompilerParams(
            collective_id=0, has_side_effects=True, vmem_limit_bytes=40 * 2**20
        ),
        cost_estimate=pl.CostEstimate(flops=6 * 10**9, bytes_accessed=12 * 10**6, transcendentals=10**6),
        name="distill",
    )(*(pltpu.with_memory_space_constraint(a, pltpu.HBM) for a in args))
    grad = jax.ShapeDtypeStruct((1, STUD, WIDTH), BF16)
    return pl.pallas_call(
        products,
        out_shape=(grad, grad, grad),
        in_specs=[vmem] * 4,
        out_specs=(anym,) * 3,
        scratch_shapes=[V((2, 2, STUD, HALF), BF16), pltpu.SemaphoreType.DMA((3, 2))],
        compiler_params=pltpu.CompilerParams(vmem_limit_bytes=16 * 2**20),
        cost_estimate=pl.CostEstimate(flops=15 * 10**8, bytes_accessed=3 * 10**6, transcendentals=0),
        name="products",
    )(*parts)


def solution(mesh):
    split = P(("neuron", "expert"), "dp")
    expert = P("expert", "neuron", "dp")
    return jax.shard_map(
        body,
        mesh=mesh,
        in_specs=(split, split, split, split, expert, expert, expert, P(), P()),
        out_specs=(expert, expert, expert),
        check_vma=False,
    )
```

```python
import jax
import jax.numpy as jnp
from jax import lax
from jax.experimental import pallas as pl
from jax.experimental.pallas import tpu as pltpu
from jax.sharding import PartitionSpec as P

MESH = pl.DeviceIdType.MESH
F32, BF16 = jnp.float32, jnp.bfloat16
NX, NY, NZ = 4, 4, 8
ROWS = 16
WIDTH, HALF = 2048, 1024
TEACH, STUD = 448, 224
TQ, SQ = 112, 64
HQ = TQ + SQ
CHUNK, PARTS, SLABS = 128, 4, 2
TOKENS = CHUNK * PARTS
ORDER = (0, 1, 7, 2, 6, 3, 5, 4)
POS = tuple(ORDER.index(k) for k in range(NZ))
PC = 256
ZSEND = ((7,), (1, 6), (2, 5), (3, 4))
NSEM = 192
DRELAY = (0, 0, 0, 0)
DIRECT = (0, 0, 1, 1)
RELAY = (1, 1, 1, 1)
NT = (((1,), (1,)), ((), ()))


PROGRAM = (
    "X0 Q1A.0 Q1A.2 P1A ",
    "Q1A.3 Q1A.1 LD1 SA.0 ",
    "P2A.0 P2A.2 P2A.3 LD2 ",
    "SA.2 KA.0 SA.3 P2A.1 ",
    "SA.1 O.0 B.0 KA.2 ",
    "O.2 B.2 KA.3 R.0 ",
    "KA.1 O.3 B.3 R.2 ",
    "O.1 B.1 R.3 MIX ",
    "A.2 R.1 A.3 E.2 ",
    "A.1 A.0 E.3 F1.2 ",
    "F1.3 E.1 E.0 F1.1 ",
    "F1.0 F2.3 F2.2 F2.1 ",
    "FP FAC F2.0 WS ",
    "FQ Q1G.0 FF P1G ",
    "Q1G.1 Q1G.2 Q1G.3 WS ",
    "SG.0 P2G.0 P2G.1 SG.1 ",
    "P2G.2 P2G.3 SG.2 KG.0 ",
    "HO.0 H.0 SG.3 KG.1 ",
    "HO.1 KG.2 HO.2 H.1 ",
    "HS.0 H.2 KG.3 HO.3 ",
    "HS.1 H.3 HM WS ",
    "SL.1 SL.0 GD SL.2 ",
    "SL.3 ",
)


def dot(a, b, dims=(((1,), (0,)), ((), ()))):
    return lax.dot_general(a, b, dims, preferred_element_type=F32)


def kernel(
    tokens, routes, weights, tgate, tup, tdown, sgate, sup, sdown,
    tok, gd, pgrad, lgrad,
    res, hm, tin, rin, win, w1, wd, tf, blk, mix, bacc, psend, prec, pass_on, hall, fac,
    fcore, rcore, facc, fsend, rz, ry, qsend, rqz, ysend, rpy,
    isend, irec, iall, iown, hgrad, lsem, ssem, rsem,
):
    ix, iz, ie = lax.axis_index("dp"), lax.axis_index("neuron"), lax.axis_index("expert")
    iy, ic = ie // 2, lax.rem(ie, 2)
    oc = 1 - ic

    def dev(x=0, y=0, z=0, c=0):
        core = oc if c else ic
        return (lax.rem(ix + x, NX), lax.rem(iz + z, NZ), lax.rem(iy + y, NY) * 2 + core)

    partners = (
        [dev(x=k) for k in range(1, NX)] + [dev(y=k) for k in range(1, NY)]
        + [dev(z=k) for k in range(1, NZ)] + [dev(c=1)]
    )
    barrier = pltpu.get_barrier_semaphore()
    for p in partners:
        pl.semaphore_signal(barrier, inc=1, device_id=p, device_id_type=MESH)

    loads = []

    def load(src, dst):
        cp = pltpu.make_async_copy(src, dst, lsem.at[len(loads)])
        cp.start()
        loads.append(cp)

    load(tokens, tin)
    load(routes, rin)
    load(weights, win)
    n_w1, n_all = 3 + 8 * NX, 3 + 12 * NX

    def load_first():
        zero = jnp.zeros((SQ // 2, HALF), BF16)
        for h in range(2):
            w1[h, 3, TQ + 32:HQ] = zero
            w1[h, 3, HQ + TQ + 32:] = zero
        for j in range(NX):
            n = SQ if j < 3 else SQ // 2
            for h in range(2):
                cols = pl.ds(h * HALF, HALF)
                load(tgate.at[pl.ds(j * TQ, TQ), cols], w1.at[h, j, pl.ds(0, TQ)])
                load(sgate.at[0, pl.ds(j * SQ, n), cols], w1.at[h, j, pl.ds(TQ, n)])
                load(tup.at[pl.ds(j * TQ, TQ), cols], w1.at[h, j, pl.ds(HQ, TQ)])
                load(sup.at[0, pl.ds(j * SQ, n), cols], w1.at[h, j, pl.ds(HQ + TQ, n)])

    def load_down():
        zero = jnp.zeros((SQ // 2, HALF), BF16)
        for h in range(2):
            wd[h, 3, TQ + 32:HQ] = zero
        for j in range(NX):
            n = SQ if j < 3 else SQ // 2
            for h in range(2):
                cols = pl.ds(h * HALF, HALF)
                load(tdown.at[pl.ds(j * TQ, TQ), cols], wd.at[h, j, pl.ds(0, TQ)])
                load(sdown.at[0, pl.ds(j * SQ, n), cols], wd.at[h, j, pl.ds(TQ, n)])

    loaded = set()

    def weights_ready(first, last):
        for i in range(first, last):
            if i not in loaded:
                loaded.add(i)
                loads[i].wait()

    weights_ready(0, 3)

    for h in range(2):
        tf[h] = tin[:, h * HALF:(h + 1) * HALF].astype(F32)
    blk[pl.ds(pl.multiple_of(ic * 8, 8), 8), :] = tf[ic]
    pl.semaphore_wait(barrier, len(partners))

    sent = []

    def send(src, dst, to):
        i = len(sent)
        cp = pltpu.make_async_remote_copy(
            src_ref=src, dst_ref=dst, send_sem=ssem.at[i], recv_sem=rsem.at[i],
            device_id=to, device_id_type=MESH,
        )
        cp.start()
        sent.append(cp)
        return cp

    landed = set()

    left_off = [0]

    def finish(spare):
        last = max(len(sent) - spare, left_off[0])
        for cp in sent[left_off[0]:last]:
            cp.wait_send()
        left_off[0] = last

    def arrived(copies):
        for c in copies:
            if id(c) not in landed:
                landed.add(id(c))
                c.wait_recv()

    def exchange():
        cp = send(tf.at[oc], blk.at[pl.ds(pl.multiple_of(ic * 8, 8), 8), :], dev(c=1))
        cp.wait_recv()
        tok[ic, 0, 0:ROWS] = blk[...].astype(BF16)

    pcols, qcols = pl.ds(0, PC), pl.ds(PC, HALF - PC)

    def rows(k):
        return pl.ds((k % NY) * ROWS, ROWS)

    def group(part):
        return pl.ds(part * SLABS, SLABS)

    cps = {}

    def gather_tasks(buf, name):
        own = buf.at[ic, 0, pl.ds(0, ROWS)]

        def y_first():
            for key, cols in (("P1", pcols), ("PQ", qcols)):
                cps[key + name] = [
                    send(own.at[:, cols], buf.at[ic, 0, rows(-k), cols], dev(y=k)) for k in (2, 1, 3)
                ]

        def z_first(part):
            cps["Q1" + name, part] = [
                send(own.at[:, qcols], buf.at[ic, POS[-k % NZ], pl.ds(0, ROWS), qcols], dev(z=k)) for k in ZSEND[part]
            ]

        def y_then_z(part):
            arrived(cps.pop("P1" + name, []))
            cps["P2" + name, part] = [
                send(buf.at[ic, 0, :, pcols], buf.at[ic, POS[-k % NZ], :, pcols], dev(z=k)) for k in ZSEND[part]
            ]

        def z_then_y(part):
            arrived(cps["Q1" + name, part])
            g = group(part) if part else pl.ds(1, SLABS - 1)
            cps["S" + name, part] = [
                send(buf.at[ic, g, pl.ds(0, ROWS), qcols], buf.at[ic, g, rows(-k), qcols], dev(y=k)) for k in (2, 1, 3)
            ]

        def to_core(part):
            arrived(cps["P2" + name, part])
            arrived(cps["S" + name, part])
            if part == 0:
                arrived(cps["PQ" + name])
            cps["K" + name, part] = [send(buf.at[ic, group(part)], buf.at[ic, group(part)], dev(c=1))]

        return {"P1": y_first, "Q1": z_first, "P2": y_then_z, "S": z_then_y, "K": to_core}

    def piece(buf, h, part):
        return buf[h, part * SLABS:(part + 1) * SLABS].reshape(CHUNK, HALF)

    def own_half(part):
        weights_ready(3, n_w1)
        arrived(cps["P2A", part])
        arrived(cps["SA", part])
        if part == 0:
            arrived(cps["PQA"])
        for d in range(NX):
            bacc[part, d] = dot(w1[ic, lax.rem(ix + d, NX)], piece(tok, ic, part), NT)

    def hidden_parts(part):
        arrived(cps["KA", part])
        out = []
        for d in (2, 1, 3, 0):
            val = bacc[part, d] + dot(w1[oc, lax.rem(ix + d, NX)], piece(tok, oc, part), NT)
            if d == 0 or (RELAY[part] and d != 2):
                bacc[part, d] = val
                continue
            psend[part, d] = val.astype(BF16)
            if RELAY[part]:
                cps["R", part] = [
                    send(psend.at[part, d, pl.ds(0, HQ)], pass_on.at[part, 0], dev(x=1)),
                    send(psend.at[part, d, pl.ds(HQ, HQ)], pass_on.at[part, 1], dev(x=3)),
                ]
            else:
                out.append(send(psend.at[part, d], prec.at[part, NX - d], dev(x=d)))
        cps["B", part] = out

    def relay(part):
        arrived(cps["R", part])
        for n, d in enumerate((1, 3)):
            mid = slice(n * HQ, n * HQ + HQ)
            rest = slice(HQ - n * HQ, 2 * HQ - n * HQ)
            psend[part, d, mid] = (bacc[part, d, mid] + pass_on[part, n].astype(F32)).astype(BF16)
            psend[part, d, rest] = bacc[part, d, rest].astype(BF16)
            cps["B", part].append(send(psend.at[part, d], prec.at[part, NX - d], dev(x=d)))

    def activate(part):
        arrived(cps["B", part])
        total = bacc[part, 0]
        for d in (1, 3) if RELAY[part] else (1, 2, 3):
            total = total + prec[part, d].astype(F32)
        pre, lift = total[:HQ], total[HQ:]
        s = jax.nn.sigmoid(pre)
        act = pre * s
        hidden = act * lift
        weight = mix[part, 0:1]
        hall[part, ix, 0:TQ] = (-hidden[:TQ]).astype(BF16)
        hall[part, ix, TQ:HQ] = (hidden[TQ:] * weight).astype(BF16)
        mine = hall.at[part, ix]
        cps["A", part] = [send(mine, mine, dev(x=d)) for d in ((1, 3) if DRELAY[part] else (2, 1, 3))]
        slope = s * (1.0 + pre * (1.0 - s))
        fac[ix, part, 0] = (weight * (lift * slope)[TQ:]).astype(BF16)
        fac[ix, part, 1] = (weight * act[TQ:]).astype(BF16)

    def factors():
        cps["FAC"] = [send(fac.at[ix], fac.at[ix], dev(x=k)) for k in (2, 1, 3)]

    def pass_hidden(part):
        arrived(cps["A", part])
        cps["DR", part] = []
        for d, first, n in ((1, 0, 96), (3, 96, HQ - 96)):
            piece_of = hall.at[part, lax.rem(ix + NX - d, NX), pl.ds(first, n)]
            cps["DR", part].append(send(piece_of, piece_of, dev(x=d)))

    def outputs(part):
        weights_ready(n_w1, n_all)
        arrived(cps["A", part])
        arrived(cps.get(("DR", part), []))
        hidden = hall[part].reshape(NX * HQ, CHUNK).T
        fcore[part] = dot(hidden, wd[oc].reshape(NX * HQ, HALF)).astype(BF16)
        cps["E", part] = [send(fcore.at[part], rcore.at[part], dev(c=1))]
        facc[part] = dot(hidden, wd[ic].reshape(NX * HQ, HALF))

    def scatter_first(part):
        arrived(cps["E", part])
        total = facc[part] + rcore[part].astype(F32)
        facc[part] = total
        fsend[part * SLABS:(part + 1) * SLABS] = total.astype(BF16).reshape(SLABS, 64, HALF)
        cps["F1", part] = [
            send(fsend.at[group(part), rows(k), qcols], ry.at[part, NY - k], dev(y=k)) for k in (2, 1, 3)
        ]
        cps["F1P", part] = [
            send(fsend.at[pos, :, pcols], rz.at[POS[-ORDER[pos] % NZ]], dev(z=ORDER[pos]))
            for pos in range(part * SLABS, (part + 1) * SLABS) if ORDER[pos]
        ]

    def scatter_second(part):
        arrived(cps["F1", part])
        total = facc[part].reshape(SLABS, 64, HALF)[:, :ROWS, PC:]
        for d in range(1, NY):
            total = total + ry[part, d].astype(F32)
        if part == 0:
            ysend[0:ROWS, PC:] = total[0]
        qsend[part * SLABS:(part + 1) * SLABS] = total.astype(BF16)
        cps["F2", part] = [
            send(qsend.at[pos], rqz.at[POS[-ORDER[pos] % NZ]], dev(z=ORDER[pos]))
            for pos in range(part * SLABS, (part + 1) * SLABS) if ORDER[pos]
        ]

    def scatter_y():
        total = facc[0, 0:64, :PC]
        for part in range(PARTS):
            arrived(cps["F1P", part])
        for pos in range(1, NZ):
            total = total + rz[pos].astype(F32)
        ysend[:, :PC] = total
        rpy[0] = total.astype(BF16)
        cps["FP"] = [send(rpy.at[0, rows(k)], rpy.at[NY - k, pl.ds(0, ROWS)], dev(y=k)) for k in (2, 1, 3)]

    def residual_q():
        for part in range(PARTS):
            arrived(cps["F2", part])
        total = ysend[0:ROWS, PC:]
        for pos in range(1, NZ):
            total = total + rqz[pos].astype(F32)
        res[ic, 0, 0:ROWS, PC:] = total.astype(BF16)

    def residual_p():
        arrived(cps["FP"])
        total = ysend[0:ROWS, :PC]
        for k in range(1, NY):
            total = total + rpy[k, 0:ROWS].astype(F32)
        res[ic, 0, 0:ROWS, :PC] = total.astype(BF16)

    def mixing():
        m = jnp.sum(jnp.where(rin[...] == ie, win[...], 0.0), axis=0, keepdims=True)
        m = jnp.broadcast_to(m, (8, TOKENS))
        m = pltpu.roll(m, lax.rem(NZ - iz, NZ) * 64, 1)
        lane = lax.broadcasted_iota(jnp.int32, (8, TOKENS), 1)
        near = pltpu.roll(m, lax.rem(TOKENS - iy * ROWS, TOKENS), 1)
        far = pltpu.roll(m, 64 - iy * ROWS, 1)
        m = jnp.where(lax.rem(lane, 64) < 64 - iy * ROWS, near, far)
        low = lax.broadcasted_iota(jnp.int32, (8, CHUNK), 1) < 64
        for part in range(PARTS):
            two = []
            for side in range(2):
                k = ORDER[part * 2 + side]
                t = m[:, (k // 2) * CHUNK:(k // 2 + 1) * CHUNK]
                two.append(t if k % 2 == side else pltpu.roll(t, 64, 1))
            mix[part] = jnp.where(low, two[0], two[1])

    def own_hidden_grads(part):
        left = wd[ic, :, TQ:].reshape(NX * SQ, HALF)
        iown[part] = dot(left, piece(res, ic, part), NT).reshape(NX, SQ, CHUNK)

    def hidden_grads(part):
        arrived(cps["KG", part])
        left = wd[oc, :, TQ:].reshape(NX * SQ, HALF)
        val = iown[part].reshape(NX * SQ, CHUNK) + dot(left, piece(res, oc, part), NT)
        iown[part] = val.reshape(NX, SQ, CHUNK)
        isend[part] = val.astype(BF16).reshape(NX, SQ, CHUNK)
        if DIRECT[part]:
            out = [send(isend.at[part], iall.at[part, NX - d], dev(x=d)) for d in (2, 1, 3)]
        else:
            out = [
                send(isend.at[part, lax.rem(ix + d, NX)], irec.at[part, NX - d], dev(x=d)) for d in (2, 1, 3)
            ]
        cps["H", part] = out

    def hidden_sum(part):
        arrived(cps["H", part])
        total = iown[part, ix]
        for d in range(1, NX):
            total = total + irec[part, d].astype(F32)
        hgrad[part, ix] = total.astype(BF16)
        mine = hgrad.at[part, ix]
        cps["HS", part] = [send(mine, mine, dev(x=d)) for d in (2, 1, 3)]

    def slopes(part):
        arrived(cps["H" if DIRECT[part] else "HS", part])
        arrived(cps["FAC"])
        cols = pl.ds(part * CHUNK, CHUNK)
        if DIRECT[part]:
            grad = iown[part].reshape(NX * SQ, CHUNK)
            for d in range(1, NX):
                grad = grad + iall[part, d].reshape(NX * SQ, CHUNK).astype(F32)
            pgrad[:, cols] = (grad * fac[:, part, 0].reshape(NX * SQ, CHUNK).astype(F32)).astype(BF16)
            lgrad[:, cols] = (grad * fac[:, part, 1].reshape(NX * SQ, CHUNK).astype(F32)).astype(BF16)
            return
        for j in range(NX):
            grad = hgrad[part, j].astype(F32)
            units = pl.ds(j * SQ, SQ)
            pgrad[units, cols] = (grad * fac[j, part, 0].astype(F32)).astype(BF16)
            lgrad[units, cols] = (grad * fac[j, part, 1].astype(F32)).astype(BF16)

    def weighted_hidden():
        for part in range(PARTS):
            for j in range(NX):
                hm[j * SQ:(j + 1) * SQ, part * CHUNK:(part + 1) * CHUNK] = hall[part, j, TQ:HQ]

    def down_product():
        for h in range(2):
            gd[h] = dot(hm[:STUD], res[h].reshape(TOKENS, HALF)).astype(BF16)

    tasks = {
        "X0": exchange, "MIX": mixing, "HM": weighted_hidden, "FAC": factors,
        "WS": lambda: finish(12), "LD1": load_first, "LD2": load_down, "DR": pass_hidden, "GD": down_product,
        "O": own_half, "B": hidden_parts, "R": relay, "A": activate, "E": outputs, "F1": scatter_first,
        "F2": scatter_second, "FP": scatter_y, "FQ": residual_q, "FF": residual_p, "HO": own_hidden_grads, "H": hidden_grads,
        "HS": hidden_sum, "SL": slopes,
    }
    for name, buf in (("A", tok), ("G", res)):
        tasks.update({key + name: task for key, task in gather_tasks(buf, name).items()})
    for step in ("".join(PROGRAM)).split():
        key, _, part = step.partition(".")
        tasks[key](*([int(part)] if part else []))
    finish(0)


def products(tok, gd, pgrad, lgrad, ggate, gup, gdown, stage, sem):
    copies = []

    def write(src, out, n, h):
        cp = pltpu.make_async_copy(src, out.at[0, :, pl.ds(h * HALF, HALF)], sem.at[n, h])
        cp.start()
        copies.append(cp)

    for h in range(2):
        write(gd.at[h], gdown, 2, h)
    for n, (left, out) in enumerate(((pgrad, ggate), (lgrad, gup))):
        for h in range(2):
            stage[n, h] = dot(left[:STUD], tok[h].reshape(TOKENS, HALF)).astype(BF16)
            write(stage.at[n, h], out, n, h)
    for cp in copies:
        cp.wait()


def body(tokens, tgate, tup, tdown, sgate, sup, sdown, routes, route_weight):
    vmem, anym = pl.BlockSpec(memory_space=pltpu.VMEM), pl.BlockSpec(memory_space=pl.ANY)
    V = pltpu.VMEM
    held = (
        V((2, NZ, 64, HALF), BF16),
        V((2, STUD, HALF), BF16),
        V((NX * SQ, TOKENS), BF16),
        V((NX * SQ, TOKENS), BF16),
    )
    args = (tokens, routes.T, route_weight.T, tgate, tup, tdown, sgate, sup, sdown)
    parts = pl.pallas_call(
        kernel,
        out_shape=held,
        in_specs=[anym] * 9,
        out_specs=(vmem,) * 4,
        scratch_shapes=[
            V((2, NZ, 64, HALF), BF16),
            V((NX * SQ, TOKENS), BF16),
            V((8, WIDTH), BF16),
            V((2, TOKENS), jnp.int32),
            V((2, TOKENS), F32),
            V((2, NX, 2 * HQ, HALF), BF16),
            V((2, NX, HQ, HALF), BF16),
            V((2, 8, HALF), F32),
            V((ROWS, HALF), F32),
            V((PARTS, 8, CHUNK), F32),
            V((PARTS, NX, 2 * HQ, CHUNK), F32),
            V((PARTS, NX, 2 * HQ, CHUNK), BF16),
            V((PARTS, NX, 2 * HQ, CHUNK), BF16),
            V((PARTS, 2, HQ, CHUNK), BF16),
            V((PARTS, NX, HQ, CHUNK), BF16),
            V((NX, PARTS, 2, SQ, CHUNK), BF16),
            V((PARTS, CHUNK, HALF), BF16),
            V((PARTS, CHUNK, HALF), BF16),
            V((PARTS, CHUNK, HALF), F32),
            V((NZ, 64, HALF), BF16),
            V((NZ, 64, PC), BF16),
            V((PARTS, NY, SLABS, ROWS, HALF - PC), BF16),
            V((NZ, ROWS, HALF - PC), BF16),
            V((NZ, ROWS, HALF - PC), BF16),
            V((64, HALF), F32),
            V((NY, 64, PC), BF16),
            V((PARTS, NX, SQ, CHUNK), BF16),
            V((PARTS, NX, SQ, CHUNK), BF16),
            V((PARTS, NX, NX, SQ, CHUNK), BF16),
            V((PARTS, NX, SQ, CHUNK), F32),
            V((PARTS, NX, SQ, CHUNK), BF16),
            pltpu.SemaphoreType.DMA((64,)),
            pltpu.SemaphoreType.DMA((NSEM,)),
            pltpu.SemaphoreType.DMA((NSEM,)),
        ],
        compiler_params=pltpu.CompilerParams(
            collective_id=0, has_side_effects=True, vmem_limit_bytes=40 * 2**20
        ),
        cost_estimate=pl.CostEstimate(flops=6 * 10**9, bytes_accessed=12 * 10**6, transcendentals=10**6),
        name="distill",
    )(*(pltpu.with_memory_space_constraint(a, pltpu.HBM) for a in args))
    grad = jax.ShapeDtypeStruct((1, STUD, WIDTH), BF16)
    return pl.pallas_call(
        products,
        out_shape=(grad, grad, grad),
        in_specs=[vmem] * 4,
        out_specs=(anym,) * 3,
        scratch_shapes=[V((2, 2, STUD, HALF), BF16), pltpu.SemaphoreType.DMA((3, 2))],
        compiler_params=pltpu.CompilerParams(vmem_limit_bytes=16 * 2**20),
        cost_estimate=pl.CostEstimate(flops=15 * 10**8, bytes_accessed=3 * 10**6, transcendentals=0),
        name="products",
    )(*parts)


def solution(mesh):
    split = P(("neuron", "expert"), "dp")
    expert = P("expert", "neuron", "dp")
    return jax.shard_map(
        body,
        mesh=mesh,
        in_specs=(split, split, split, split, expert, expert, expert, P(), P()),
        out_specs=(expert, expert, expert),
        check_vma=False,
    )
```
